32 devices in a mesh: harm: 8 (over z, x), remap: 4 (over y, core).
Axes of the slice: x: 2, y: 2, z: 4, core: 2. Of those that a mesh axis runs over, the one named last changes fastest.
Arguments:
- alm: bfloat16 [4096, 32, 4096], P(('harm', 'remap')), may hold values from -0.125 to 0.125
- legendre: bfloat16 [4096, 8, 4096], P(('harm', 'remap')), may hold values from -0.09375 to 0.09375
- src_cycle: int32 [8, 8192], P('harm', 'remap'), may hold values from 0 to 6, as said below
- src_phi: int32 [8, 8192], P('harm', 'remap'), may hold values from 0 to 8191, as said below
- off_cycle: int32 [8, 8192], P('harm', 'remap'), may hold values from 0 to 15
- off_phi: int32 [8, 8192], P('harm', 'remap'), may hold values from 0 to 15
Outputs:
- lensed: bfloat16 [16, 8, 8192], P(None, 'harm', 'remap')
The draws below stay inside these ranges and needn't reach their ends.
Inputs may be any that keep to these rules, and one draw needn't show every extreme that they name: The pixel on cycle r has src_cycle = r + d clipped to 0 to 6, with d from -3 to 2. The pixel at position p of its cycle has src_phi = (p + d) mod 8192, with d from -8 to 7.
All inputs are finite; a program needn't handle non-finite values.
Results may differ from the reference program's by a relative error of at most 0.0015.
Values sent between devices are 32-bit elements; how exact they have to be, the bound alone decides.
A program may use at most 128 MiB of HBM per device.

```python
import math
import jax
import jax.numpy as jnp
from jax import lax

L = 4096
M = 4096
NPHI = 8192
SIMS = 16
DR = 3
DP = 8
QF = 16
CYCLES = 8


def draw_src_cycle(key, part):
    cycle_steps = jax.random.randint(jax.random.fold_in(key, 11), (CYCLES, NPHI), -DR, DR)
    cycle_rows = lax.broadcasted_iota(jnp.int32, (CYCLES, NPHI), 0)
    return jnp.clip(cycle_rows + cycle_steps, 0, CYCLES - 2).astype(jnp.int32)


def draw_src_phi(key, part):
    phi_steps = jax.random.randint(jax.random.fold_in(key, 23), (CYCLES, NPHI), -DP, DP)
    phi_columns = lax.broadcasted_iota(jnp.int32, (CYCLES, NPHI), 1)
    return ((phi_columns + phi_steps) % NPHI).astype(jnp.int32)


def plant(entries, own_key, low, top_value):
    spot = [jax.random.randint(jax.random.fold_in(own_key, axis), (), 0, length) for axis, length in enumerate(entries.shape)]
    widest = entries.shape.index(max(entries.shape))
    next_to = spot[:widest] + [(spot[widest] + 1) % entries.shape[widest]] + spot[widest + 1:]
    return entries.at[tuple(spot)].set(low).at[tuple(next_to)].set(top_value)


def levels(stream_key, extent, split, smallest, largest):
    def one(position, blocks):
        steps = jax.random.uniform(jax.random.fold_in(jax.random.fold_in(stream_key, 6), position), (blocks,), jnp.float32, smallest / len(split), largest / len(split))
        return jnp.repeat(jnp.exp(steps), extent[position] // blocks).reshape((-1,) + (1,) * (len(extent) - position - 1))

    loudness = one(*split[0])
    for cut in split[1:]:
        loudness = loudness * one(*cut)
    return loudness


def gaussian(key, extent, deviation, reach, shards=(), dtype=jnp.bfloat16):
    loudness = levels(key, extent, shards, -0.22, 0.18) if shards else 1.0
    array = jax.random.normal(key, extent, jnp.float32) * deviation * loudness
    return jnp.minimum(jnp.maximum(array, -reach), reach).astype(dtype)


def setup_inputs(seed: int = 0) -> dict:
    arg_keys = jax.random.split(jax.random.key(seed), 7)
    return {
        "alm": gaussian(arg_keys[0], (M, 2 * SIMS, L), ((4 * M) ** -0.5), 0.125, ((0, 32),)),
        "legendre": gaussian(arg_keys[1], (M, CYCLES, L), L ** -0.5, 0.09375, ((0, 32),)),
        "src_cycle": draw_src_cycle(jax.random.fold_in(arg_keys[6], 71), 0),
        "src_phi": draw_src_phi(jax.random.fold_in(arg_keys[6], 71), 0),
        "off_cycle": plant(jax.random.randint(arg_keys[4], (CYCLES, NPHI), 0, QF), jax.random.fold_in(arg_keys[4], 1), 0, QF - 1).astype(jnp.int32),
        "off_phi": plant(jax.random.randint(arg_keys[5], (CYCLES, NPHI), 0, QF), jax.random.fold_in(arg_keys[5], 1), 0, QF - 1).astype(jnp.int32),
    }


def reference(alm, legendre, src_cycle, src_phi, off_cycle, off_phi):
    block_size = math.gcd(M, 256)
    alm_blocks = alm.reshape(M // block_size, block_size, 2 * SIMS, L)
    table_blocks = legendre.reshape(M // block_size, block_size, CYCLES, L)

    def synth_block(pair):
        coeffs, values = pair
        return jnp.einsum("mkl,mrl->krm", coeffs.astype(jnp.float32), values.astype(jnp.float32))

    pieces = lax.map(synth_block, (alm_blocks, table_blocks))
    harmonic = jnp.transpose(pieces, (1, 2, 0, 3)).reshape(2 * SIMS, CYCLES, M)
    spectrum = harmonic[:SIMS] + 1j * harmonic[SIMS:]
    unlensed = (NPHI * jnp.fft.irfft(spectrum, n=NPHI, axis=-1)).astype(jnp.float32)
    cycle_frac = off_cycle.astype(jnp.float32) / QF
    phi_frac = off_phi.astype(jnp.float32) / QF
    next_phi = (src_phi + 1) % NPHI
    next_cycle = src_cycle + 1
    near_row = (1.0 - phi_frac) * unlensed[:, src_cycle, src_phi] + phi_frac * unlensed[:, src_cycle, next_phi]
    far_row = (1.0 - phi_frac) * unlensed[:, next_cycle, src_phi] + phi_frac * unlensed[:, next_cycle, next_phi]
    lensed = (1.0 - cycle_frac) * near_row + cycle_frac * far_row
    return lensed.astype(jnp.bfloat16)
```

```python
import math

import functools

import jax
import jax.numpy as jnp
import ml_dtypes
import numpy as np
from jax import lax
from jax.experimental import pallas as pl
from jax.experimental.pallas import tpu as pltpu
from jax.sharding import PartitionSpec as P

DR = 3
DP = 8
QF = 16


def with_halo(cells, sides, width):
    for axis, dim in sides:
        count = lax.axis_size(axis)
        head = lax.slice_in_dim(cells, 0, width, axis=dim)
        tail = lax.slice_in_dim(cells, cells.shape[dim] - width, cells.shape[dim], axis=dim)
        cells = jnp.concatenate(
            [
                lax.ppermute(tail, axis, [(i, (i + 1) % count) for i in range(count)]),
                cells,
                lax.ppermute(head, axis, [((i + 1) % count, i) for i in range(count)]),
            ],
            axis=dim,
        )
    return cells


def from_behind(block, axis, distance):
    devices = range(lax.axis_size(axis))
    route = [(i - distance, i) for i in devices if i - distance in devices]
    return lax.ppermute(block, axis, route)


def phase_table(rows, cols, factor, phi_count):
    row_ids = lax.broadcasted_iota(jnp.int32, (rows, cols), 0)
    col_ids = lax.broadcasted_iota(jnp.int32, (rows, cols), 1)
    phase = factor * row_ids * col_ids % phi_count
    angles = phase.astype(jnp.float32) * (2.0 * math.pi / phi_count)
    return (jnp.cos(angles), jnp.sin(angles))


def synthesize(full_coeffs, count, phi_count, sim_count):
    cycle_dev = full_coeffs.shape[0]
    order_count = full_coeffs.shape[2]
    inner = 64
    outer = order_count // inner
    period = phi_count // inner
    order_ids = lax.iota(jnp.int32, order_count)
    weights = jnp.where(order_ids == 0, 1.0, 2.0).astype(jnp.float32)
    scaled = full_coeffs * weights
    real_part = scaled[:, :sim_count].reshape(cycle_dev * sim_count, outer, inner)
    imag_part = scaled[:, sim_count:].reshape(cycle_dev * sim_count, outer, inner)
    first_cos, first_sin = phase_table(outer, period, inner, phi_count)
    high = lax.Precision.HIGHEST
    section_re = jnp.einsum("kba,bu->kau", real_part, first_cos, precision=high) - jnp.einsum(
        "kba,bu->kau", imag_part, first_sin, precision=high
    )
    section_im = jnp.einsum("kba,bu->kau", real_part, first_sin, precision=high) + jnp.einsum(
        "kba,bu->kau", imag_part, first_cos, precision=high
    )
    twist_cos, twist_sin = phase_table(inner, period, 1, phi_count)
    turned_re = section_re * twist_cos - section_im * twist_sin
    turned_im = section_re * twist_sin + section_im * twist_cos
    second_cos, second_sin = phase_table(inner, inner, period, phi_count)
    values = jnp.einsum("kau,av->kvu", turned_re, second_cos, precision=high) - jnp.einsum(
        "kau,av->kvu", turned_im, second_sin, precision=high
    )
    cycle_values = values.reshape(cycle_dev * sim_count, phi_count)
    return jnp.transpose(cycle_values.reshape(cycle_dev, sim_count, count), (1, 0, 2))


def general_body(alm, legendre, src_cycle, src_phi, off_cycle, off_phi):
    sim_count = alm.shape[1] // 2
    n_harm = lax.axis_size("harm")
    n_remap = lax.axis_size("remap")
    m_local = alm.shape[0]
    cycle_dev = src_cycle.shape[0]
    quarter = src_cycle.shape[1]
    phi_count = quarter * n_remap
    harm_index = lax.axis_index("harm")
    remap_index = lax.axis_index("remap")
    harmonic = jnp.einsum("mkl,mrl->rkm", alm, legendre, preferred_element_type=jnp.float32)
    cycle_coeffs = lax.all_to_all(harmonic, "harm", split_axis=0, concat_axis=2, tiled=True)
    group_ids = lax.iota(jnp.int32, n_remap)
    picker = jnp.where(group_ids == remap_index, 1.0, 0.0).astype(jnp.float32)
    spread = cycle_coeffs.reshape(cycle_dev, 2 * sim_count, n_harm, 1, m_local) * picker[:, None]
    full_coeffs = spread.reshape(cycle_dev, 2 * sim_count, n_harm * n_remap * m_local)
    partial_map = synthesize(full_coeffs, phi_count, phi_count, sim_count)
    unlensed = lax.psum_scatter(partial_map, "remap", scatter_dimension=2, tiled=True)
    widened = with_halo(unlensed, (("remap", 2),), DP)
    reach_devices = -(-DR // cycle_dev)
    below_parts = [
        from_behind(widened, "harm", distance) for distance in range(reach_devices, 0, -1)
    ]
    above_parts = [
        from_behind(widened, "harm", -distance) for distance in range(1, reach_devices + 1)
    ]
    window = jnp.concatenate(below_parts + [widened] + above_parts, axis=1)
    cycle_base = harm_index * cycle_dev - reach_devices * cycle_dev
    phi_base = remap_index * quarter - DP
    span = window.shape[2]
    cycle_slot = src_cycle - cycle_base
    phi_slot = (src_phi - phi_base) % phi_count
    flat_index = (cycle_slot * span + phi_slot).reshape(-1)
    flattened = window.reshape(sim_count, -1)

    def tap_values(offset):
        return jnp.take(flattened, flat_index + offset, axis=1)

    cycle_frac = (off_cycle.astype(jnp.float32) / QF).reshape(-1)
    phi_frac = (off_phi.astype(jnp.float32) / QF).reshape(-1)
    near_row = (1.0 - phi_frac) * tap_values(0) + phi_frac * tap_values(1)
    far_row = (1.0 - phi_frac) * tap_values(span) + phi_frac * tap_values(span + 1)
    mixed = (1.0 - cycle_frac) * near_row + cycle_frac * far_row
    return mixed.reshape(sim_count, cycle_dev, quarter).astype(jnp.bfloat16)


LANES = 128


def split_bf16(table):
    high = table.astype(ml_dtypes.bfloat16)
    low = (table - high.astype(np.float64)).astype(ml_dtypes.bfloat16)
    return high, low


def tables(n_harm, n_remap, phi_count):
    groups = n_harm * n_remap
    period = phi_count // LANES
    order = (np.arange(n_harm)[None, :] * n_remap + np.arange(n_remap)[:, None]).reshape(-1)
    angle = 2.0 * np.pi * ((np.arange(period)[:, None] * order[None, :]) % period) / period
    first = np.block([[np.cos(angle), -np.sin(angle)], [np.sin(angle), np.cos(angle)]])
    high, low = split_bf16(first)
    first_table = np.concatenate([high, high, low], axis=1)
    angle = 2.0 * np.pi * np.arange(LANES)[:, None] * np.arange(LANES)[None, :] / phi_count
    twist = np.stack([np.cos(angle), np.sin(angle)]).astype(np.float32)
    blocks = np.arange(-8, period + 8) % period
    angle = 2.0 * np.pi * ((blocks[:, None] * np.arange(LANES)[None, :]) % period) / period
    high, low = split_bf16(2.0 * np.concatenate([np.cos(angle), -np.sin(angle)], axis=1))
    second_table = np.stack([high, low])
    return first_table, twist, second_table


def accumulate_orders(group, alm_ref, leg_ref, acc_ref):
    per_group, _, rows, depth = alm_ref.shape
    cycles = leg_ref.shape[2]
    coeffs = alm_ref[...].reshape(per_group * rows, depth)
    basis = leg_ref[...].reshape(per_group * cycles, depth)
    product = lax.dot_general(
        coeffs, basis, (((1,), (1,)), ((), ())), preferred_element_type=jnp.float32
    )
    lane = lax.broadcasted_iota(jnp.int32, (rows, LANES), 1)
    own = jnp.zeros((rows, LANES), jnp.float32)
    for i in range(per_group):
        own = jnp.where(lane // cycles == i, product[i * rows : (i + 1) * rows], own)
    device = lax.axis_index("harm") * lax.axis_size("remap") + lax.axis_index("remap")
    first_order = jnp.logical_and(device == 0, group == 0)
    for r in range(cycles):
        turned = pltpu.roll(own, lax.rem(group - r + LANES, LANES), axis=1)
        turned = jnp.where(jnp.logical_and(first_order, lane == 0), 0.5 * turned, turned)
        held = acc_ref[r * rows : (r + 1) * rows, :]
        acc_ref[r * rows : (r + 1) * rows, :] = jnp.where(lane % cycles == group, turned, held)


def dot_last(a, b):
    return lax.dot_general(a, b, (((1,), (1,)), ((), ())), preferred_element_type=jnp.float32)


def synthesize_sim(x_ref, e, per_dev, cycles, first_ref, twist_ref, second, z_ref):
    step = per_dev * 2 * cycles
    groups = x_ref.shape[0] // step
    half = first_ref.shape[0] // 2
    columns = []
    for r in range(cycles):
        columns.append(
            jnp.concatenate(
                [
                    x_ref[pl.ds((e * 2 + c) * cycles + r, groups, stride=step), :]
                    for c in range(2)
                ],
                axis=0,
            )
        )
    coeffs = jnp.concatenate(columns, axis=1)
    high = coeffs.astype(jnp.bfloat16)
    low = (coeffs - high.astype(jnp.float32)).astype(jnp.bfloat16)
    section = jnp.dot(
        first_ref[...].astype(jnp.bfloat16),
        jnp.concatenate([high, low, high], axis=0),
        preferred_element_type=jnp.float32,
    )
    for r in range(cycles):
        re = section[:half, r * LANES : (r + 1) * LANES]
        im = section[half:, r * LANES : (r + 1) * LANES]
        re = jnp.concatenate([re] * (LANES // half), axis=0)
        im = jnp.concatenate([im] * (LANES // half), axis=0)
        turned = jnp.concatenate(
            [
                re * twist_ref[0] - im * twist_ref[1],
                re * twist_ref[1] + im * twist_ref[0],
            ],
            axis=1,
        )
        turned_high = turned.astype(jnp.bfloat16)
        z_ref[0, r * LANES : (r + 1) * LANES, :] = turned_high
        z_ref[1, r * LANES : (r + 1) * LANES, :] = (
            turned - turned_high.astype(jnp.float32)
        ).astype(jnp.bfloat16)
    span = second.shape[0] // 2
    both = dot_last(second, z_ref[0])
    return both[:span] + both[span:] + dot_last(second[:span], z_ref[1])


def interpolate(e, r, cycles, u_ref, sc, sp, oc, op, tiles):
    lane = lax.broadcasted_iota(jnp.int32, (tiles, LANES), 1)
    near_index = sp & (LANES - 1)
    far_index = (sp + 1) & (LANES - 1)
    b = op.astype(jnp.float32) * (1.0 / QF)
    a = oc.astype(jnp.float32) * (1.0 / QF)
    total = jnp.zeros((tiles, LANES), jnp.float32)
    for j in range(max(0, r - DR), min(cycles - 1, r + DR) + 1):
        left = u_ref[e, 0, j]
        right = u_ref[e, 1, j]

        def tap(index):
            return jnp.where(
                lane < LANES // 2,
                jnp.take_along_axis(left, index, axis=1, mode="promise_in_bounds"),
                jnp.take_along_axis(right, index, axis=1, mode="promise_in_bounds"),
            )

        weight = jnp.where(sc == j, 1.0 - a, 0.0) + jnp.where(sc == j - 1, a, 0.0)
        total = total + weight * ((1.0 - b) * tap(near_index) + b * tap(far_index))
    return total


def to_device(src, dst, send_sem, recv_sem, axis, index):
    return pltpu.make_async_remote_copy(
        src_ref=src,
        dst_ref=dst,
        send_sem=send_sem,
        recv_sem=recv_sem,
        device_id={axis: index},
        device_id_type=pl.DeviceIdType.MESH,
    )


def sky_step(
    n_harm, n_remap, per_dev,
    alm_ref, leg_ref, sc_ref, sp_ref, oc_ref, op_ref, first_ref, twist_ref, second_ref,
    out_ref,
    acc_ref, pack_ref, x_ref, where_ref, z_ref, w_ref, u_ref, maps_ref, fin_ref,
    i_send, i_recv, a_send, a_recv, y_send, y_recv, s_send, s_recv, f_send, f_recv, o_send, o_recv,
):
    group = pl.program_id(0)
    cycles = leg_ref.shape[2]
    tiles = sc_ref.shape[0]
    rows = alm_ref.shape[2]
    piece = per_dev * 2 * cycles
    me = lax.axis_index("harm")
    q = lax.axis_index("remap")
    across = lax.rem(q + 2, n_remap)
    sibling = q + 1 - 2 * lax.rem(q, 2)
    far = lax.rem(sibling + 2, n_remap)
    peers = [lax.rem(me + k, n_harm) for k in range(1, n_harm)]

    def slot(quarter, source):
        start = pl.multiple_of((quarter * n_harm + source) * piece, piece)
        return x_ref.at[pl.ds(start, piece), :]

    def packed(target):
        return pack_ref.at[pl.ds(pl.multiple_of(target * piece, piece), piece), :]

    def index_copy(source, target):
        return to_device(
            where_ref.at[source], where_ref.at[source], i_send.at[target], i_recv.at[source], "harm", target
        )

    def order_copy(source, target):
        return to_device(
            packed(target), slot(q, source), a_send.at[target], a_recv.at[source], "harm", target
        )

    def across_copy(quarter, source):
        return to_device(
            slot(quarter, source), slot(quarter, source), y_send.at[source], y_recv.at[source], "remap", across
        )

    def sibling_copy(quarter, source):
        return to_device(
            slot(quarter, source), slot(quarter, source), s_send.at[source], s_recv.at[source], "remap", sibling
        )

    def forward_copy(quarter, source):
        return to_device(
            slot(quarter, source), slot(quarter, source), f_send.at[source], f_recv.at[source], "remap", sibling
        )

    def map_copy(source, target):
        return to_device(
            maps_ref.at[target], fin_ref.at[source], o_send.at[target], o_recv.at[source], "harm", target
        )

    @pl.when(group == 0)
    def _():
        barrier = pltpu.get_barrier_semaphore()
        for p in peers:
            pl.semaphore_signal(
                barrier, inc=1, device_id={"harm": p}, device_id_type=pl.DeviceIdType.MESH
            )
        for p in (across, sibling):
            pl.semaphore_signal(
                barrier, inc=1, device_id={"remap": p}, device_id_type=pl.DeviceIdType.MESH
            )
        for i, ref in enumerate((sc_ref, sp_ref, oc_ref, op_ref)):
            where_ref[me, i] = ref[...]
        pl.semaphore_wait(barrier, n_harm + 1)
        for p in peers:
            index_copy(me, p).start()

    accumulate_orders(group, alm_ref, leg_ref, acc_ref)

    @pl.when(group == pl.num_programs(0) - 1)
    def _():
        sims = rows // 2
        for k in range(rows):
            sim, part = k % sims, k // sims
            start = (sim // per_dev) * piece + (sim % per_dev) * 2 * cycles + part * cycles
            pack_ref[start : start + cycles, :] = acc_ref[pl.ds(k, cycles, stride=rows), :]
        for p in reversed(peers):
            order_copy(me, p).start()
        own = pl.multiple_of((q * n_harm + me) * piece, piece)
        x_ref[pl.ds(own, piece), :] = pack_ref[pl.ds(pl.multiple_of(me * piece, piece), piece), :]
        across_copy(q, me).start()
        sibling_copy(q, me).start()
        for p in peers:
            order_copy(p, p).wait_recv()
            across_copy(q, p).start()
            sibling_copy(q, p).start()
        for p in [me] + peers:
            across_copy(across, p).wait_recv()
            forward_copy(across, p).start()
        for p in peers:
            index_copy(p, p).wait_recv()
        for p in [me] + peers:
            sibling_copy(sibling, p).wait_recv()
        for p in [me] + peers:
            forward_copy(far, p).wait_recv()

        start = pl.multiple_of(q * tiles, tiles)
        span = tiles + 16
        second = jnp.concatenate(
            [second_ref[0, pl.ds(start, span), :], second_ref[1, pl.ds(start, span), :]], axis=0
        ).astype(jnp.bfloat16)
        lane = lax.broadcasted_iota(jnp.int32, (tiles, LANES), 1)
        for e in range(per_dev):
            w_ref[...] = synthesize_sim(
                x_ref, e, per_dev, cycles, first_ref, twist_ref, second, z_ref
            )
            for j in range(cycles):
                cols = slice(j * LANES, (j + 1) * LANES)
                here = w_ref[8 : 8 + tiles, cols]
                u_ref[e, 0, j] = jnp.where(lane >= 3 * LANES // 4, w_ref[7 : 7 + tiles, cols], here)
                u_ref[e, 1, j] = jnp.where(lane < LANES // 4, w_ref[9 : 9 + tiles, cols], here)
        for r in range(cycles):
            for e in range(per_dev):
                maps_ref[r, e] = interpolate(
                    e, r, cycles, u_ref,
                    where_ref[r, 0], where_ref[r, 1], where_ref[r, 2], where_ref[r, 3], tiles,
                )

            @pl.when(me != r)
            def _():
                map_copy(me, r).start()

        fin_ref[me] = maps_ref[me]
        for p in peers:
            map_copy(p, p).wait_recv()
        for s in range(sims):
            for t in range(tiles):
                out_ref[s : s + 1, t * LANES : (t + 1) * LANES] = fin_ref[
                    s // per_dev, s % per_dev, t : t + 1
                ].astype(jnp.bfloat16)
        for p in peers:
            index_copy(me, p).wait_send()
            order_copy(me, p).wait_send()
            map_copy(me, p).wait_send()
        for p in [me] + peers:
            across_copy(q, p).wait_send()
            sibling_copy(q, p).wait_send()
            forward_copy(across, p).wait_send()


def body(alm, legendre, src_cycle, src_phi, off_cycle, off_phi):
    n_harm = lax.axis_size("harm")
    n_remap = lax.axis_size("remap")
    m_local, rows, depth = alm.shape
    sims = rows // 2
    per_dev = sims // n_harm
    cycles = legendre.shape[1]
    quarter = src_cycle.shape[1]
    tiles = quarter // LANES
    per_group = LANES // cycles
    groups = m_local // per_group
    piece = per_dev * 2 * cycles
    first_table, twist, second_table = tables(n_harm, n_remap, quarter * n_remap)
    whole = pl.BlockSpec(memory_space=pltpu.VMEM)
    sems = [pltpu.SemaphoreType.DMA((n_harm,)) for _ in range(12)]
    lensed = pl.pallas_call(
        functools.partial(sky_step, n_harm, n_remap, per_dev),
        grid=(groups,),
        in_specs=[
            pl.BlockSpec((per_group, 1, rows, depth), lambda g: (0, g, 0, 0)),
            pl.BlockSpec((per_group, 1, cycles, depth), lambda g: (0, g, 0, 0)),
        ]
        + [whole] * 7,
        out_specs=whole,
        out_shape=jax.ShapeDtypeStruct((sims, quarter), jnp.bfloat16),
        scratch_shapes=[
            pltpu.VMEM((rows * cycles, LANES), jnp.float32),
            pltpu.VMEM((rows * cycles, LANES), jnp.float32),
            pltpu.VMEM((n_remap * n_harm * piece, LANES), jnp.float32),
            pltpu.VMEM((n_harm, 4, tiles, LANES), jnp.int32),
            pltpu.VMEM((2, cycles * LANES, 2 * LANES), jnp.bfloat16),
            pltpu.VMEM((tiles + 16, cycles * LANES), jnp.float32),
            pltpu.VMEM((per_dev, 2, cycles, tiles, LANES), jnp.float32),
            pltpu.VMEM((cycles, per_dev, tiles, LANES), jnp.float32),
            pltpu.VMEM((n_harm, per_dev, tiles, LANES), jnp.float32),
        ]
        + sems,
        compiler_params=pltpu.CompilerParams(
            collective_id=0, has_side_effects=True, vmem_limit_bytes=56 * 2**20
        ),
    )(
        alm.reshape(per_group, groups, rows, depth),
        legendre.reshape(per_group, groups, cycles, depth),
        *(array.reshape(tiles, LANES) for array in (src_cycle, src_phi, off_cycle, off_phi)),
        jnp.asarray(first_table.astype(np.float32)),
        jnp.asarray(twist),
        jnp.asarray(second_table.astype(np.float32)),
    )
    return lensed.reshape(sims, 1, quarter)


def fits(mesh, alm, legendre, src_cycle):
    n_harm, n_remap = mesh.shape["harm"], mesh.shape["remap"]
    cycles = legendre.shape[1]
    sims = alm.shape[1] // 2
    phi_count = src_cycle.shape[1]
    return (
        cycles == n_harm == 8
        and sims % n_harm == 0
        and alm.shape[0] == LANES * n_harm * n_remap
        and phi_count == LANES * 64
        and (phi_count // n_remap) % (16 * LANES) == 0
        and (n_harm * n_remap) % 8 == 0
        and n_remap == 4
    )


def solution(mesh):
    def run(*arrays):
        chosen = body if fits(mesh, arrays[0], arrays[1], arrays[2]) else general_body
        return sharded(mesh, chosen)(*arrays)

    return run


def sharded(mesh, chosen):
    return jax.shard_map(
        chosen,
        mesh=mesh,
        in_specs=(
            P(("harm", "remap"), None, None),
            P(("harm", "remap"), None, None),
            P("harm", "remap"),
            P("harm", "remap"),
            P("harm", "remap"),
            P("harm", "remap"),
        ),
        out_specs=P(None, "harm", "remap"),
        check_vma=False,
    )
```

```python
import math

import functools

import jax
import jax.numpy as jnp
import ml_dtypes
import numpy as np
from jax import lax
from jax.experimental import pallas as pl
from jax.experimental.pallas import tpu as pltpu
from jax.sharding import PartitionSpec as P

DR = 3
DP = 8
QF = 16


def with_halo(cells, sides, width):
    for axis, dim in sides:
        count = lax.axis_size(axis)
        head = lax.slice_in_dim(cells, 0, width, axis=dim)
        tail = lax.slice_in_dim(cells, cells.shape[dim] - width, cells.shape[dim], axis=dim)
        cells = jnp.concatenate(
            [
                lax.ppermute(tail, axis, [(i, (i + 1) % count) for i in range(count)]),
                cells,
                lax.ppermute(head, axis, [((i + 1) % count, i) for i in range(count)]),
            ],
            axis=dim,
        )
    return cells


def from_behind(block, axis, distance):
    devices = range(lax.axis_size(axis))
    route = [(i - distance, i) for i in devices if i - distance in devices]
    return lax.ppermute(block, axis, route)


def phase_table(rows, cols, factor, phi_count):
    row_ids = lax.broadcasted_iota(jnp.int32, (rows, cols), 0)
    col_ids = lax.broadcasted_iota(jnp.int32, (rows, cols), 1)
    phase = factor * row_ids * col_ids % phi_count
    angles = phase.astype(jnp.float32) * (2.0 * math.pi / phi_count)
    return (jnp.cos(angles), jnp.sin(angles))


def synthesize(full_coeffs, count, phi_count, sim_count):
    cycle_dev = full_coeffs.shape[0]
    order_count = full_coeffs.shape[2]
    inner = 64
    outer = order_count // inner
    period = phi_count // inner
    order_ids = lax.iota(jnp.int32, order_count)
    weights = jnp.where(order_ids == 0, 1.0, 2.0).astype(jnp.float32)
    scaled = full_coeffs * weights
    real_part = scaled[:, :sim_count].reshape(cycle_dev * sim_count, outer, inner)
    imag_part = scaled[:, sim_count:].reshape(cycle_dev * sim_count, outer, inner)
    first_cos, first_sin = phase_table(outer, period, inner, phi_count)
    high = lax.Precision.HIGHEST
    section_re = jnp.einsum("kba,bu->kau", real_part, first_cos, precision=high) - jnp.einsum(
        "kba,bu->kau", imag_part, first_sin, precision=high
    )
    section_im = jnp.einsum("kba,bu->kau", real_part, first_sin, precision=high) + jnp.einsum(
        "kba,bu->kau", imag_part, first_cos, precision=high
    )
    twist_cos, twist_sin = phase_table(inner, period, 1, phi_count)
    turned_re = section_re * twist_cos - section_im * twist_sin
    turned_im = section_re * twist_sin + section_im * twist_cos
    second_cos, second_sin = phase_table(inner, inner, period, phi_count)
    values = jnp.einsum("kau,av->kvu", turned_re, second_cos, precision=high) - jnp.einsum(
        "kau,av->kvu", turned_im, second_sin, precision=high
    )
    cycle_values = values.reshape(cycle_dev * sim_count, phi_count)
    return jnp.transpose(cycle_values.reshape(cycle_dev, sim_count, count), (1, 0, 2))


def general_body(alm, legendre, src_cycle, src_phi, off_cycle, off_phi):
    sim_count = alm.shape[1] // 2
    n_harm = lax.axis_size("harm")
    n_remap = lax.axis_size("remap")
    m_local = alm.shape[0]
    cycle_dev = src_cycle.shape[0]
    quarter = src_cycle.shape[1]
    phi_count = quarter * n_remap
    harm_index = lax.axis_index("harm")
    remap_index = lax.axis_index("remap")
    harmonic = jnp.einsum("mkl,mrl->rkm", alm, legendre, preferred_element_type=jnp.float32)
    cycle_coeffs = lax.all_to_all(harmonic, "harm", split_axis=0, concat_axis=2, tiled=True)
    group_ids = lax.iota(jnp.int32, n_remap)
    picker = jnp.where(group_ids == remap_index, 1.0, 0.0).astype(jnp.float32)
    spread = cycle_coeffs.reshape(cycle_dev, 2 * sim_count, n_harm, 1, m_local) * picker[:, None]
    full_coeffs = spread.reshape(cycle_dev, 2 * sim_count, n_harm * n_remap * m_local)
    partial_map = synthesize(full_coeffs, phi_count, phi_count, sim_count)
    unlensed = lax.psum_scatter(partial_map, "remap", scatter_dimension=2, tiled=True)
    widened = with_halo(unlensed, (("remap", 2),), DP)
    reach_devices = -(-DR // cycle_dev)
    below_parts = [
        from_behind(widened, "harm", distance) for distance in range(reach_devices, 0, -1)
    ]
    above_parts = [
        from_behind(widened, "harm", -distance) for distance in range(1, reach_devices + 1)
    ]
    window = jnp.concatenate(below_parts + [widened] + above_parts, axis=1)
    cycle_base = harm_index * cycle_dev - reach_devices * cycle_dev
    phi_base = remap_index * quarter - DP
    span = window.shape[2]
    cycle_slot = src_cycle - cycle_base
    phi_slot = (src_phi - phi_base) % phi_count
    flat_index = (cycle_slot * span + phi_slot).reshape(-1)
    flattened = window.reshape(sim_count, -1)

    def tap_values(offset):
        return jnp.take(flattened, flat_index + offset, axis=1)

    cycle_frac = (off_cycle.astype(jnp.float32) / QF).reshape(-1)
    phi_frac = (off_phi.astype(jnp.float32) / QF).reshape(-1)
    near_row = (1.0 - phi_frac) * tap_values(0) + phi_frac * tap_values(1)
    far_row = (1.0 - phi_frac) * tap_values(span) + phi_frac * tap_values(span + 1)
    mixed = (1.0 - cycle_frac) * near_row + cycle_frac * far_row
    return mixed.reshape(sim_count, cycle_dev, quarter).astype(jnp.bfloat16)


LANES = 128


def split_bf16(table):
    high = table.astype(ml_dtypes.bfloat16)
    low = (table - high.astype(np.float64)).astype(ml_dtypes.bfloat16)
    return high, low


def tables(n_harm, n_remap, phi_count):
    lane = np.arange(LANES)
    order = (lane // 8) * 4 + lane % 4
    parity = (lane // 4) % 2
    device = (np.arange(n_harm)[None, :] * n_remap + np.arange(n_remap)[:, None]).reshape(-1)
    block = (device[:, None] * 2 + np.arange(2)[None, :]).reshape(-1)
    angle = 2.0 * np.pi * ((np.arange(LANES)[:, None] * block[None, :]) % LANES) / LANES
    first = np.block([[np.cos(angle), -np.sin(angle)], [np.sin(angle), np.cos(angle)]])
    high, low = split_bf16(first)
    first_table = np.concatenate([high, high, low], axis=1).astype(np.float32)
    angle = 2.0 * np.pi * np.arange(LANES)[:, None] * order[None, :] / phi_count
    twist = np.stack([np.cos(angle), np.sin(angle)]).astype(np.float32)
    period = phi_count // LANES
    rows = np.arange(-8, period + 8) % period
    angle = 2.0 * np.pi * ((rows[:, None] * order[None, :]) % period) / period
    second = 2.0 * np.concatenate([np.cos(angle), -np.sin(angle)], axis=1)
    keep = np.concatenate([parity, parity])[None, None, :] == np.arange(2)[:, None, None]
    high, low = split_bf16(np.where(keep, second[None], 0.0))
    second_table = np.concatenate([high, low]).astype(np.float32)
    return first_table, twist, second_table


def accumulate_orders(half, turn, alm_ref, leg_ref, acc_ref):
    _, per_group, _, rows, depth = alm_ref.shape
    cycles = leg_ref.shape[3]
    coeffs = alm_ref[...].reshape(per_group * rows, depth)
    basis = leg_ref[...].reshape(per_group * cycles, depth)
    product = lax.dot_general(
        coeffs, basis, (((1,), (1,)), ((), ())), preferred_element_type=jnp.float32
    )
    lane = lax.broadcasted_iota(jnp.int32, (rows, LANES), 1)
    own = jnp.zeros((rows, LANES), jnp.float32)
    for i in range(per_group):
        own = jnp.where(lane // cycles == i, product[i * rows : (i + 1) * rows], own)
    device = lax.axis_index("harm") * lax.axis_size("remap") + lax.axis_index("remap")
    first_order = jnp.logical_and(device == 0, jnp.logical_and(half == 0, turn == 0))
    for r in range(cycles):
        place = 4 * (r % 2) + turn
        turned = pltpu.roll(own, lax.rem(place - r + LANES, LANES), axis=1)
        turned = jnp.where(jnp.logical_and(first_order, lane == place), 0.5 * turned, turned)
        at = (r // 2) * rows
        acc_ref[at : at + rows, :] = jnp.where(
            lane % cycles == place, turned, acc_ref[at : at + rows, :]
        )


def dot_last(a, b):
    return lax.dot_general(a, b, (((1,), (1,)), ((), ())), preferred_element_type=jnp.float32)


def synthesize_sim(x_ref, e, step, pairs, first, twist_ref, second, z_ref):
    blocks = x_ref.shape[0] // step
    columns = []
    for pair in range(pairs):
        columns.append(
            jnp.concatenate(
                [
                    x_ref[pl.ds((e * 2 + c) * pairs + pair, blocks, stride=step), :]
                    for c in range(2)
                ],
                axis=0,
            )
        )
    coeffs = jnp.concatenate(columns, axis=1)
    high = coeffs.astype(jnp.bfloat16)
    low = (coeffs - high.astype(jnp.float32)).astype(jnp.bfloat16)
    section = jnp.dot(
        first, jnp.concatenate([high, low, high], axis=0), preferred_element_type=jnp.float32
    )
    for pair in range(pairs):
        cols = slice(pair * LANES, (pair + 1) * LANES)
        re = section[:LANES, cols]
        im = section[LANES:, cols]
        turned = jnp.concatenate(
            [
                re * twist_ref[0] - im * twist_ref[1],
                re * twist_ref[1] + im * twist_ref[0],
            ],
            axis=1,
        )
        turned_high = turned.astype(jnp.bfloat16)
        z_ref[0, cols, :] = turned_high
        z_ref[1, cols, :] = (turned - turned_high.astype(jnp.float32)).astype(jnp.bfloat16)
    span = second.shape[0] // 2
    both = dot_last(second, z_ref[0])
    return both[:span] + both[span:] + dot_last(second[:span], z_ref[1])


def interpolate(r, cycles, per_dev, u_ref, sc, sp, oc, op, tiles):
    lane = lax.broadcasted_iota(jnp.int32, (tiles, LANES), 1)
    near_index = sp & (LANES - 1)
    far_index = (sp + 1) & (LANES - 1)
    b = op.astype(jnp.float32) * (1.0 / QF)
    a = oc.astype(jnp.float32) * (1.0 / QF)
    totals = [jnp.zeros((tiles, LANES), jnp.float32) for _ in range(per_dev)]
    for j in range(max(0, r - DR), min(cycles - 1, r + DR) + 1):
        weight = jnp.where(sc == j, 1.0 - a, jnp.where(sc == j - 1, a, 0.0))
        near_weight = weight * (1.0 - b)
        far_weight = weight * b
        for e in range(per_dev):
            left = u_ref[e, 0, j]
            right = u_ref[e, 1, j]
            near, far = (
                jnp.where(
                    lane < LANES // 2,
                    jnp.take_along_axis(left, index, axis=1, mode="promise_in_bounds"),
                    jnp.take_along_axis(right, index, axis=1, mode="promise_in_bounds"),
                )
                for index in (near_index, far_index)
            )
            totals[e] = totals[e] + near_weight * near + far_weight * far
    return totals


def to_device(src, dst, send_sem, recv_sem, axis, index):
    return pltpu.make_async_remote_copy(
        src_ref=src,
        dst_ref=dst,
        send_sem=send_sem,
        recv_sem=recv_sem,
        device_id={axis: index},
        device_id_type=pl.DeviceIdType.MESH,
    )


def sky_step(
    n_harm, n_remap, per_dev,
    alm_ref, leg_ref, sc_ref, sp_ref, oc_ref, op_ref, first_ref, twist_ref, second_ref,
    out_ref,
    acc_ref, pack_ref, x_ref, where_ref, z_ref, w_ref, u_ref, maps_ref, fin_ref,
    i_send, i_recv, a_send, a_recv, y_send, y_recv, s_send, s_recv, f_send, f_recv, o_send, o_recv,
):
    group = pl.program_id(0)
    groups = pl.num_programs(0)
    turns = groups // 2
    cycles = leg_ref.shape[3]
    pairs = cycles // 2
    tiles = sc_ref.shape[0]
    rows = alm_ref.shape[3]
    sims = rows // 2
    piece = per_dev * 2 * pairs
    me = lax.axis_index("harm")
    q = lax.axis_index("remap")
    across = lax.rem(q + 2, n_remap)
    sibling = q + 1 - 2 * lax.rem(q, 2)
    far = lax.rem(sibling + 2, n_remap)
    peers = [lax.rem(me + k, n_harm) for k in range(1, n_harm)]

    def slot(half, quarter, source):
        start = pl.multiple_of(((quarter * n_harm + source) * 2 + half) * piece, piece)
        return x_ref.at[pl.ds(start, piece), :]

    def packed(half, target):
        return pack_ref.at[half, pl.ds(pl.multiple_of(target * piece, piece), piece), :]

    def index_copy(source, target):
        return to_device(
            where_ref.at[source], where_ref.at[source], i_send.at[target], i_recv.at[source], "harm", target
        )

    def order_copy(half, source, target):
        return to_device(
            packed(half, target), slot(half, q, source),
            a_send.at[half, target], a_recv.at[half, source], "harm", target,
        )

    def across_copy(half, quarter, source):
        held = slot(half, quarter, source)
        return to_device(held, held, y_send.at[half, source], y_recv.at[half, source], "remap", across)

    def sibling_copy(half, quarter, source):
        held = slot(half, quarter, source)
        return to_device(held, held, s_send.at[half, source], s_recv.at[half, source], "remap", sibling)

    def forward_copy(half, quarter, source):
        held = slot(half, quarter, source)
        return to_device(held, held, f_send.at[half, source], f_recv.at[half, source], "remap", sibling)

    def map_copy(source, target):
        return to_device(
            maps_ref.at[target], fin_ref.at[source], o_send.at[target], o_recv.at[source], "harm", target
        )

    def send_orders(half):
        for k in range(rows):
            sim, part = k % sims, k // sims
            start = (sim // per_dev) * piece + ((sim % per_dev) * 2 + part) * pairs
            pack_ref[half, start : start + pairs, :] = acc_ref[pl.ds(k, pairs, stride=rows), :]
        for p in peers:
            order_copy(half, me, p).start()
        own = pl.multiple_of(((q * n_harm + me) * 2 + half) * piece, piece)
        mine = pl.multiple_of(me * piece, piece)
        x_ref[pl.ds(own, piece), :] = pack_ref[half, pl.ds(mine, piece), :]
        across_copy(half, q, me).start()
        sibling_copy(half, q, me).start()

    def relay_orders(half):
        for p in peers:
            order_copy(half, p, p).wait_recv()
            across_copy(half, q, p).start()
            sibling_copy(half, q, p).start()

    def forward_orders(half):
        for p in [me] + peers:
            across_copy(half, across, p).wait_recv()
            forward_copy(half, across, p).start()

    @pl.when(group == 0)
    def _():
        barrier = pltpu.get_barrier_semaphore()
        for p in peers:
            pl.semaphore_signal(
                barrier, inc=1, device_id={"harm": p}, device_id_type=pl.DeviceIdType.MESH
            )
        for p in (across, sibling):
            pl.semaphore_signal(
                barrier, inc=1, device_id={"remap": p}, device_id_type=pl.DeviceIdType.MESH
            )
        for i, ref in enumerate((sc_ref, sp_ref, oc_ref, op_ref)):
            where_ref[me, i] = ref[...]
        pl.semaphore_wait(barrier, n_harm + 1)
        for p in peers:
            index_copy(me, p).start()

    accumulate_orders(group // turns, lax.rem(group, turns), alm_ref, leg_ref, acc_ref)

    @pl.when(group == turns - 1)
    def _():
        send_orders(0)

    @pl.when(group == turns + 1)
    def _():
        relay_orders(0)

    @pl.when(group == turns + 2)
    def _():
        forward_orders(0)

    @pl.when(group == groups - 1)
    def _():
        send_orders(1)
        relay_orders(1)
        forward_orders(1)
        for p in peers:
            index_copy(p, p).wait_recv()
        for half in range(2):
            for p in [me] + peers:
                sibling_copy(half, sibling, p).wait_recv()
                forward_copy(half, far, p).wait_recv()

        start = pl.multiple_of(q * tiles, tiles)
        span = tiles + 16
        second = jnp.concatenate(
            [second_ref[i, pl.ds(start, span), :] for i in range(4)], axis=0
        ).astype(jnp.bfloat16)
        first = first_ref[...].astype(jnp.bfloat16)
        lane = lax.broadcasted_iota(jnp.int32, (tiles, LANES), 1)
        for e in range(per_dev):
            w_ref[...] = synthesize_sim(x_ref, e, piece, pairs, first, twist_ref, second, z_ref)
            for j in range(cycles):
                cols = slice((j // 2) * LANES, (j // 2 + 1) * LANES)
                top = (j % 2) * span + 8
                here = w_ref[top : top + tiles, cols]
                before = w_ref[top - 1 : top - 1 + tiles, cols]
                after = w_ref[top + 1 : top + 1 + tiles, cols]
                u_ref[e, 0, j] = jnp.where(lane >= 3 * LANES // 4, before, here)
                u_ref[e, 1, j] = jnp.where(lane < LANES // 4, after, here)
        for r in range(cycles):
            totals = interpolate(
                r, cycles, per_dev, u_ref,
                where_ref[r, 0], where_ref[r, 1], where_ref[r, 2], where_ref[r, 3], tiles,
            )
            for e in range(per_dev):
                maps_ref[r, e * tiles : (e + 1) * tiles, :] = totals[e]

            @pl.when(me != r)
            def _():
                map_copy(me, r).start()

        fin_ref[me] = maps_ref[me]
        for p in peers:
            map_copy(p, p).wait_recv()
        for t in range(tiles):
            out_ref[:, t * LANES : (t + 1) * LANES] = jnp.concatenate(
                [fin_ref[h, pl.ds(t, per_dev, stride=tiles), :] for h in range(n_harm)], axis=0
            ).astype(jnp.bfloat16)
        for p in peers:
            index_copy(me, p).wait_send()
            map_copy(me, p).wait_send()
        for half in range(2):
            for p in peers:
                order_copy(half, me, p).wait_send()
            for p in [me] + peers:
                across_copy(half, q, p).wait_send()
                sibling_copy(half, q, p).wait_send()
                forward_copy(half, across, p).wait_send()


def body(alm, legendre, src_cycle, src_phi, off_cycle, off_phi):
    n_harm = lax.axis_size("harm")
    n_remap = lax.axis_size("remap")
    m_local, rows, depth = alm.shape
    sims = rows // 2
    per_dev = sims // n_harm
    cycles = legendre.shape[1]
    quarter = src_cycle.shape[1]
    tiles = quarter // LANES
    per_group = LANES // cycles
    groups = m_local // per_group
    turns = groups // 2
    pairs = cycles // 2
    piece = per_dev * 2 * pairs
    first_table, twist, second_table = tables(n_harm, n_remap, quarter * n_remap)
    whole = pl.BlockSpec(memory_space=pltpu.VMEM)
    single = pltpu.SemaphoreType.DMA((n_harm,))
    double = pltpu.SemaphoreType.DMA((2, n_harm))
    lensed = pl.pallas_call(
        functools.partial(sky_step, n_harm, n_remap, per_dev),
        grid=(groups,),
        in_specs=[
            pl.BlockSpec((1, per_group, 1, rows, depth), lambda g: (g // turns, 0, g % turns, 0, 0)),
            pl.BlockSpec((1, per_group, 1, cycles, depth), lambda g: (g // turns, 0, g % turns, 0, 0)),
        ]
        + [whole] * 7,
        out_specs=whole,
        out_shape=jax.ShapeDtypeStruct((sims, quarter), jnp.bfloat16),
        scratch_shapes=[
            pltpu.VMEM((rows * pairs, LANES), jnp.float32),
            pltpu.VMEM((2, rows * pairs, LANES), jnp.float32),
            pltpu.VMEM((n_remap * n_harm * 2 * piece, LANES), jnp.float32),
            pltpu.VMEM((n_harm, 4, tiles, LANES), jnp.int32),
            pltpu.VMEM((2, pairs * LANES, 2 * LANES), jnp.bfloat16),
            pltpu.VMEM((2 * (tiles + 16), pairs * LANES), jnp.float32),
            pltpu.VMEM((per_dev, 2, cycles, tiles, LANES), jnp.float32),
            pltpu.VMEM((cycles, per_dev * tiles, LANES), jnp.float32),
            pltpu.VMEM((n_harm, per_dev * tiles, LANES), jnp.float32),
            single, single, double, double, double, double,
            double, double, double, double, single, single,
        ],
        compiler_params=pltpu.CompilerParams(
            collective_id=0, has_side_effects=True, vmem_limit_bytes=56 * 2**20
        ),
    )(
        alm.reshape(2, per_group, turns, rows, depth),
        legendre.reshape(2, per_group, turns, cycles, depth),
        *(array.reshape(tiles, LANES) for array in (src_cycle, src_phi, off_cycle, off_phi)),
        jnp.asarray(first_table),
        jnp.asarray(twist),
        jnp.asarray(second_table),
    )
    return lensed.reshape(sims, 1, quarter)


def fits(mesh, alm, legendre, src_cycle):
    n_harm, n_remap = mesh.shape["harm"], mesh.shape["remap"]
    cycles = legendre.shape[1]
    sims = alm.shape[1] // 2
    phi_count = src_cycle.shape[1]
    return (
        cycles == n_harm == 8
        and sims % n_harm == 0
        and alm.shape[0] == LANES * n_harm * n_remap
        and phi_count == LANES * 64
        and (phi_count // n_remap) % (16 * LANES) == 0
        and (n_harm * n_remap) % 8 == 0
        and n_remap == 4
    )


def solution(mesh):
    def run(*arrays):
        chosen = body if fits(mesh, arrays[0], arrays[1], arrays[2]) else general_body
        return sharded(mesh, chosen)(*arrays)

    return run


def sharded(mesh, chosen):
    return jax.shard_map(
        chosen,
        mesh=mesh,
        in_specs=(
            P(("harm", "remap"), None, None),
            P(("harm", "remap"), None, None),
            P("harm", "remap"),
            P("harm", "remap"),
            P("harm", "remap"),
            P("harm", "remap"),
        ),
        out_specs=P(None, "harm", "remap"),
        check_vma=False,
    )
```

```python
import math

import functools

import jax
import jax.numpy as jnp
import ml_dtypes
import numpy as np
from jax import lax
from jax.experimental import pallas as pl
from jax.experimental.pallas import tpu as pltpu
from jax.sharding import PartitionSpec as P

DR = 3
DP = 8
QF = 16


def with_halo(cells, sides, width):
    for axis, dim in sides:
        count = lax.axis_size(axis)
        head = lax.slice_in_dim(cells, 0, width, axis=dim)
        tail = lax.slice_in_dim(cells, cells.shape[dim] - width, cells.shape[dim], axis=dim)
        cells = jnp.concatenate(
            [
                lax.ppermute(tail, axis, [(i, (i + 1) % count) for i in range(count)]),
                cells,
                lax.ppermute(head, axis, [((i + 1) % count, i) for i in range(count)]),
            ],
            axis=dim,
        )
    return cells


def from_behind(block, axis, distance):
    devices = range(lax.axis_size(axis))
    route = [(i - distance, i) for i in devices if i - distance in devices]
    return lax.ppermute(block, axis, route)


def phase_table(rows, cols, factor, phi_count):
    row_ids = lax.broadcasted_iota(jnp.int32, (rows, cols), 0)
    col_ids = lax.broadcasted_iota(jnp.int32, (rows, cols), 1)
    phase = factor * row_ids * col_ids % phi_count
    angles = phase.astype(jnp.float32) * (2.0 * math.pi / phi_count)
    return (jnp.cos(angles), jnp.sin(angles))


def synthesize(full_coeffs, count, phi_count, sim_count):
    cycle_dev = full_coeffs.shape[0]
    order_count = full_coeffs.shape[2]
    inner = 64
    outer = order_count // inner
    period = phi_count // inner
    order_ids = lax.iota(jnp.int32, order_count)
    weights = jnp.where(order_ids == 0, 1.0, 2.0).astype(jnp.float32)
    scaled = full_coeffs * weights
    real_part = scaled[:, :sim_count].reshape(cycle_dev * sim_count, outer, inner)
    imag_part = scaled[:, sim_count:].reshape(cycle_dev * sim_count, outer, inner)
    first_cos, first_sin = phase_table(outer, period, inner, phi_count)
    high = lax.Precision.HIGHEST
    section_re = jnp.einsum("kba,bu->kau", real_part, first_cos, precision=high) - jnp.einsum(
        "kba,bu->kau", imag_part, first_sin, precision=high
    )
    section_im = jnp.einsum("kba,bu->kau", real_part, first_sin, precision=high) + jnp.einsum(
        "kba,bu->kau", imag_part, first_cos, precision=high
    )
    twist_cos, twist_sin = phase_table(inner, period, 1, phi_count)
    turned_re = section_re * twist_cos - section_im * twist_sin
    turned_im = section_re * twist_sin + section_im * twist_cos
    second_cos, second_sin = phase_table(inner, inner, period, phi_count)
    values = jnp.einsum("kau,av->kvu", turned_re, second_cos, precision=high) - jnp.einsum(
        "kau,av->kvu", turned_im, second_sin, precision=high
    )
    cycle_values = values.reshape(cycle_dev * sim_count, phi_count)
    return jnp.transpose(cycle_values.reshape(cycle_dev, sim_count, count), (1, 0, 2))


def general_body(alm, legendre, src_cycle, src_phi, off_cycle, off_phi):
    sim_count = alm.shape[1] // 2
    n_harm = lax.axis_size("harm")
    n_remap = lax.axis_size("remap")
    m_local = alm.shape[0]
    cycle_dev = src_cycle.shape[0]
    quarter = src_cycle.shape[1]
    phi_count = quarter * n_remap
    harm_index = lax.axis_index("harm")
    remap_index = lax.axis_index("remap")
    harmonic = jnp.einsum("mkl,mrl->rkm", alm, legendre, preferred_element_type=jnp.float32)
    cycle_coeffs = lax.all_to_all(harmonic, "harm", split_axis=0, concat_axis=2, tiled=True)
    group_ids = lax.iota(jnp.int32, n_remap)
    picker = jnp.where(group_ids == remap_index, 1.0, 0.0).astype(jnp.float32)
    spread = cycle_coeffs.reshape(cycle_dev, 2 * sim_count, n_harm, 1, m_local) * picker[:, None]
    full_coeffs = spread.reshape(cycle_dev, 2 * sim_count, n_harm * n_remap * m_local)
    partial_map = synthesize(full_coeffs, phi_count, phi_count, sim_count)
    unlensed = lax.psum_scatter(partial_map, "remap", scatter_dimension=2, tiled=True)
    widened = with_halo(unlensed, (("remap", 2),), DP)
    reach_devices = -(-DR // cycle_dev)
    below_parts = [
        from_behind(widened, "harm", distance) for distance in range(reach_devices, 0, -1)
    ]
    above_parts = [
        from_behind(widened, "harm", -distance) for distance in range(1, reach_devices + 1)
    ]
    window = jnp.concatenate(below_parts + [widened] + above_parts, axis=1)
    cycle_base = harm_index * cycle_dev - reach_devices * cycle_dev
    phi_base = remap_index * quarter - DP
    span = window.shape[2]
    cycle_slot = src_cycle - cycle_base
    phi_slot = (src_phi - phi_base) % phi_count
    flat_index = (cycle_slot * span + phi_slot).reshape(-1)
    flattened = window.reshape(sim_count, -1)

    def tap_values(offset):
        return jnp.take(flattened, flat_index + offset, axis=1)

    cycle_frac = (off_cycle.astype(jnp.float32) / QF).reshape(-1)
    phi_frac = (off_phi.astype(jnp.float32) / QF).reshape(-1)
    near_row = (1.0 - phi_frac) * tap_values(0) + phi_frac * tap_values(1)
    far_row = (1.0 - phi_frac) * tap_values(span) + phi_frac * tap_values(span + 1)
    mixed = (1.0 - cycle_frac) * near_row + cycle_frac * far_row
    return mixed.reshape(sim_count, cycle_dev, quarter).astype(jnp.bfloat16)


LANES = 128


def split_bf16(table):
    high = table.astype(ml_dtypes.bfloat16)
    low = (table - high.astype(np.float64)).astype(ml_dtypes.bfloat16)
    return high, low


def tables(n_harm, n_remap, phi_count):
    lane = np.arange(LANES)
    order = lane % (LANES // 2)
    parity = lane // (LANES // 2)
    device = (np.arange(n_harm)[None, :] * n_remap + np.arange(n_remap)[:, None]).reshape(-1)
    block = (device[:, None] * 2 + np.arange(2)[None, :]).reshape(-1)
    angle = 2.0 * np.pi * ((np.arange(LANES)[:, None] * block[None, :]) % LANES) / LANES
    first = np.block([[np.cos(angle), -np.sin(angle)], [np.sin(angle), np.cos(angle)]])
    high, low = split_bf16(first)
    first_table = np.concatenate([high, high, low], axis=1).astype(np.float32)
    angle = 2.0 * np.pi * np.arange(LANES)[:, None] * order[None, :] / phi_count
    twist = np.stack([np.cos(angle), np.sin(angle)]).astype(np.float32)
    period = phi_count // LANES
    rows = np.arange(-8, period + 8) % period
    angle = 2.0 * np.pi * ((rows[:, None] * order[None, :]) % period) / period
    second = 2.0 * np.concatenate([np.cos(angle), -np.sin(angle)], axis=1)
    keep = np.concatenate([parity, parity])[None, None, :] == np.arange(2)[:, None, None]
    high, low = split_bf16(np.where(keep, second[None], 0.0))
    second_table = np.concatenate([high, low]).astype(np.float32)
    return first_table, twist, second_table


def dot_last(a, b):
    return lax.dot_general(a, b, (((1,), (1,)), ((), ())), preferred_element_type=jnp.float32)


def synthesize_sim(x_ref, e, step, pairs, first, twist_ref, second, z_ref):
    blocks = x_ref.shape[0] // step
    columns = []
    for pair in range(pairs):
        columns.append(
            jnp.concatenate(
                [
                    x_ref[pl.ds((e * 2 + c) * pairs + pair, blocks, stride=step), :]
                    for c in range(2)
                ],
                axis=0,
            )
        )
    coeffs = jnp.concatenate(columns, axis=1)
    high = coeffs.astype(jnp.bfloat16)
    low = (coeffs - high.astype(jnp.float32)).astype(jnp.bfloat16)
    section = jnp.dot(
        first, jnp.concatenate([high, low, high], axis=0), preferred_element_type=jnp.float32
    )
    for pair in range(pairs):
        cols = slice(pair * LANES, (pair + 1) * LANES)
        re = section[:LANES, cols]
        im = section[LANES:, cols]
        turned = jnp.concatenate(
            [
                re * twist_ref[0] - im * twist_ref[1],
                re * twist_ref[1] + im * twist_ref[0],
            ],
            axis=1,
        )
        turned_high = turned.astype(jnp.bfloat16)
        z_ref[0, cols, :] = turned_high
        z_ref[1, cols, :] = (turned - turned_high.astype(jnp.float32)).astype(jnp.bfloat16)
    span = second.shape[0] // 2
    both = dot_last(second, z_ref[0])
    return both[:span] + both[span:] + dot_last(second[:span], z_ref[1])


def interpolate(r, cycles, per_dev, u_ref, sc, sp, oc, op, tiles):
    lane = lax.broadcasted_iota(jnp.int32, (tiles, LANES), 1)
    near_index = sp & (LANES - 1)
    far_index = (sp + 1) & (LANES - 1)
    b = op.astype(jnp.float32) * (1.0 / QF)
    a = oc.astype(jnp.float32) * (1.0 / QF)
    totals = [jnp.zeros((tiles, LANES), jnp.float32) for _ in range(per_dev)]
    for j in range(max(0, r - DR), min(cycles - 1, r + DR) + 1):
        weight = jnp.where(sc == j, 1.0 - a, jnp.where(sc == j - 1, a, 0.0))
        near_weight = weight * (1.0 - b)
        far_weight = weight * b
        for e in range(per_dev):
            left = u_ref[e, 0, j]
            right = u_ref[e, 1, j]
            near, far = (
                jnp.where(
                    lane < LANES // 2,
                    jnp.take_along_axis(left, index, axis=1, mode="promise_in_bounds"),
                    jnp.take_along_axis(right, index, axis=1, mode="promise_in_bounds"),
                )
                for index in (near_index, far_index)
            )
            totals[e] = totals[e] + near_weight * near + far_weight * far
    return totals


def to_device(src, dst, send_sem, recv_sem, axis, index):
    return pltpu.make_async_remote_copy(
        src_ref=src,
        dst_ref=dst,
        send_sem=send_sem,
        recv_sem=recv_sem,
        device_id={axis: index},
        device_id_type=pl.DeviceIdType.MESH,
    )


def sky_step(
    n_harm, n_remap, per_dev,
    sums_ref, sc_ref, sp_ref, oc_ref, op_ref, first_ref, twist_ref, second_ref,
    out_ref,
    half_ref, pack_ref, x_ref, z_ref, w_ref, u_ref, maps_ref, fin_ref,
    a_send, a_recv, y_send, y_recv, s_send, s_recv, f_send, f_recv, o_send, o_recv,
):
    cycles, rows, _ = sums_ref.shape
    pairs = cycles // 2
    tiles = sc_ref.shape[1]
    sims = rows // 2
    half_piece = per_dev * 2 * pairs
    piece = 2 * half_piece
    me = lax.axis_index("harm")
    q = lax.axis_index("remap")
    across = lax.rem(q + 2, n_remap)
    sibling = q + 1 - 2 * lax.rem(q, 2)
    far = lax.rem(sibling + 2, n_remap)
    peers = [lax.rem(me + k, n_harm) for k in range(1, n_harm)]

    def slot(quarter, source):
        start = pl.multiple_of((quarter * n_harm + source) * piece, piece)
        return x_ref.at[pl.ds(start, piece), :]

    def packed(target):
        return pack_ref.at[pl.ds(pl.multiple_of(target * piece, piece), piece), :]

    def order_copy(source, target):
        return to_device(
            packed(target), slot(q, source), a_send.at[target], a_recv.at[source], "harm", target
        )

    def across_copy(quarter, source):
        held = slot(quarter, source)
        return to_device(held, held, y_send.at[source], y_recv.at[source], "remap", across)

    def sibling_copy(quarter, source):
        held = slot(quarter, source)
        return to_device(held, held, s_send.at[source], s_recv.at[source], "remap", sibling)

    def forward_copy(quarter, source):
        held = slot(quarter, source)
        return to_device(held, held, f_send.at[source], f_recv.at[source], "remap", sibling)

    def map_copy(source, target):
        return to_device(
            maps_ref.at[target], fin_ref.at[source], o_send.at[target], o_recv.at[source], "harm", target
        )

    barrier = pltpu.get_barrier_semaphore()
    for p in peers:
        pl.semaphore_signal(
            barrier, inc=1, device_id={"harm": p}, device_id_type=pl.DeviceIdType.MESH
        )
    for p in (across, sibling):
        pl.semaphore_signal(
            barrier, inc=1, device_id={"remap": p}, device_id_type=pl.DeviceIdType.MESH
        )
    device = me * n_remap + q
    row_lane = lax.broadcasted_iota(jnp.int32, (rows, LANES), 1)
    for pair in range(pairs):
        even, odd = sums_ref[2 * pair], sums_ref[2 * pair + 1]
        zero_order = jnp.logical_and(device == 0, row_lane == 0)
        even = jnp.where(zero_order, 0.5 * even, even)
        odd = jnp.where(zero_order, 0.5 * odd, odd)
        half_ref[pair * rows : (pair + 1) * rows, :] = jnp.where(
            row_lane < LANES // 2, even, pltpu.roll(odd, LANES // 2, axis=1)
        )
        half_ref[(pairs + pair) * rows : (pairs + pair + 1) * rows, :] = jnp.where(
            row_lane < LANES // 2, pltpu.roll(even, LANES // 2, axis=1), odd
        )
    for half in range(2):
        for k in range(rows):
            sim, part = k % sims, k // sims
            start = (sim // per_dev) * piece + half * half_piece
            start += ((sim % per_dev) * 2 + part) * pairs
            pack_ref[start : start + pairs, :] = half_ref[
                pl.ds(half * pairs * rows + k, pairs, stride=rows), :
            ]
    pl.semaphore_wait(barrier, n_harm + 1)
    for p in peers:
        order_copy(me, p).start()
    own = pl.multiple_of((q * n_harm + me) * piece, piece)
    x_ref[pl.ds(own, piece), :] = pack_ref[pl.ds(pl.multiple_of(me * piece, piece), piece), :]
    across_copy(q, me).start()
    sibling_copy(q, me).start()
    for p in peers:
        order_copy(p, p).wait_recv()
        across_copy(q, p).start()
        sibling_copy(q, p).start()
    for p in [me] + peers:
        across_copy(across, p).wait_recv()
        forward_copy(across, p).start()
    for p in [me] + peers:
        sibling_copy(sibling, p).wait_recv()
        forward_copy(far, p).wait_recv()

    start = pl.multiple_of(q * tiles, tiles)
    span = tiles + 16
    second = jnp.concatenate(
        [second_ref[i, pl.ds(start, span), :] for i in range(4)], axis=0
    ).astype(jnp.bfloat16)
    first = first_ref[...].astype(jnp.bfloat16)
    lane = lax.broadcasted_iota(jnp.int32, (tiles, LANES), 1)
    for e in range(per_dev):
        w_ref[...] = synthesize_sim(x_ref, e, half_piece, pairs, first, twist_ref, second, z_ref)
        for j in range(cycles):
            cols = slice((j // 2) * LANES, (j // 2 + 1) * LANES)
            top = (j % 2) * span + 8
            here = w_ref[top : top + tiles, cols]
            before = w_ref[top - 1 : top - 1 + tiles, cols]
            after = w_ref[top + 1 : top + 1 + tiles, cols]
            u_ref[e, 0, j] = jnp.where(lane >= 3 * LANES // 4, before, here)
            u_ref[e, 1, j] = jnp.where(lane < LANES // 4, after, here)
    for r in range(cycles):
        totals = interpolate(
            r, cycles, per_dev, u_ref,
            sc_ref[r], sp_ref[r], oc_ref[r], op_ref[r], tiles,
        )
        for e in range(per_dev):
            maps_ref[r, e * tiles : (e + 1) * tiles, :] = totals[e]

        @pl.when(me != r)
        def _():
            map_copy(me, r).start()

    fin_ref[me] = maps_ref[me]
    for p in peers:
        map_copy(p, p).wait_recv()
    for t in range(tiles):
        out_ref[:, t * LANES : (t + 1) * LANES] = jnp.concatenate(
            [fin_ref[h, pl.ds(t, per_dev, stride=tiles), :] for h in range(n_harm)], axis=0
        ).astype(jnp.bfloat16)
    for p in peers:
        order_copy(me, p).wait_send()
        map_copy(me, p).wait_send()
    for p in [me] + peers:
        across_copy(q, p).wait_send()
        sibling_copy(q, p).wait_send()
        forward_copy(across, p).wait_send()


def body(alm, legendre, src_cycle, src_phi, off_cycle, off_phi):
    n_harm = lax.axis_size("harm")
    n_remap = lax.axis_size("remap")
    rows = alm.shape[1]
    sims = rows // 2
    per_dev = sims // n_harm
    cycles = legendre.shape[1]
    quarter = src_cycle.shape[1]
    tiles = quarter // LANES
    pairs = cycles // 2
    piece = per_dev * 4 * pairs
    first_table, twist, second_table = tables(n_harm, n_remap, quarter * n_remap)
    where = [
        lax.all_gather(array, "harm", axis=0, tiled=True).reshape(cycles, tiles, LANES)
        for array in (src_cycle, src_phi, off_cycle, off_phi)
    ]
    sums = jnp.einsum("mkl,mrl->rkm", alm, legendre, preferred_element_type=jnp.float32)
    whole = pl.BlockSpec(memory_space=pltpu.VMEM)
    lensed = pl.pallas_call(
        functools.partial(sky_step, n_harm, n_remap, per_dev),
        in_specs=[whole] * 8,
        out_specs=whole,
        out_shape=jax.ShapeDtypeStruct((sims, quarter), jnp.bfloat16),
        scratch_shapes=[
            pltpu.VMEM((rows * 2 * pairs, LANES), jnp.float32),
            pltpu.VMEM((rows * 2 * pairs, LANES), jnp.float32),
            pltpu.VMEM((n_remap * n_harm * piece, LANES), jnp.float32),
            pltpu.VMEM((2, pairs * LANES, 2 * LANES), jnp.bfloat16),
            pltpu.VMEM((2 * (tiles + 16), pairs * LANES), jnp.float32),
            pltpu.VMEM((per_dev, 2, cycles, tiles, LANES), jnp.float32),
            pltpu.VMEM((cycles, per_dev * tiles, LANES), jnp.float32),
            pltpu.VMEM((n_harm, per_dev * tiles, LANES), jnp.float32),
        ]
        + [pltpu.SemaphoreType.DMA((n_harm,)) for _ in range(10)],
        compiler_params=pltpu.CompilerParams(
            collective_id=0, has_side_effects=True, vmem_limit_bytes=16 * 2**20
        ),
    )(
        sums,
        *where,
        jnp.asarray(first_table),
        jnp.asarray(twist),
        jnp.asarray(second_table),
    )
    return lensed.reshape(sims, 1, quarter)


def fits(mesh, alm, legendre, src_cycle):
    n_harm, n_remap = mesh.shape["harm"], mesh.shape["remap"]
    cycles = legendre.shape[1]
    sims = alm.shape[1] // 2
    phi_count = src_cycle.shape[1]
    return (
        cycles == n_harm == 8
        and sims % n_harm == 0
        and alm.shape[0] == LANES * n_harm * n_remap
        and phi_count == LANES * 64
        and (phi_count // n_remap) % (16 * LANES) == 0
        and (n_harm * n_remap) % 8 == 0
        and n_remap == 4
    )


def solution(mesh):
    def run(*arrays):
        chosen = body if fits(mesh, arrays[0], arrays[1], arrays[2]) else general_body
        return sharded(mesh, chosen)(*arrays)

    return run


def sharded(mesh, chosen):
    return jax.shard_map(
        chosen,
        mesh=mesh,
        in_specs=(
            P(("harm", "remap"), None, None),
            P(("harm", "remap"), None, None),
            P("harm", "remap"),
            P("harm", "remap"),
            P("harm", "remap"),
            P("harm", "remap"),
        ),
        out_specs=P(None, "harm", "remap"),
        check_vma=False,
    )
```

```python
import math

import functools

import jax
import jax.numpy as jnp
import ml_dtypes
import numpy as np
from jax import lax
from jax.experimental import pallas as pl
from jax.experimental.pallas import tpu as pltpu
from jax.sharding import PartitionSpec as P

DR = 3
DP = 8
QF = 16


def with_halo(cells, sides, width):
    for axis, dim in sides:
        count = lax.axis_size(axis)
        head = lax.slice_in_dim(cells, 0, width, axis=dim)
        tail = lax.slice_in_dim(cells, cells.shape[dim] - width, cells.shape[dim], axis=dim)
        cells = jnp.concatenate(
            [
                lax.ppermute(tail, axis, [(i, (i + 1) % count) for i in range(count)]),
                cells,
                lax.ppermute(head, axis, [((i + 1) % count, i) for i in range(count)]),
            ],
            axis=dim,
        )
    return cells


def from_behind(block, axis, distance):
    devices = range(lax.axis_size(axis))
    route = [(i - distance, i) for i in devices if i - distance in devices]
    return lax.ppermute(block, axis, route)


def phase_table(rows, cols, factor, phi_count):
    row_ids = lax.broadcasted_iota(jnp.int32, (rows, cols), 0)
    col_ids = lax.broadcasted_iota(jnp.int32, (rows, cols), 1)
    phase = factor * row_ids * col_ids % phi_count
    angles = phase.astype(jnp.float32) * (2.0 * math.pi / phi_count)
    return (jnp.cos(angles), jnp.sin(angles))


def synthesize(full_coeffs, count, phi_count, sim_count):
    cycle_dev = full_coeffs.shape[0]
    order_count = full_coeffs.shape[2]
    inner = 64
    outer = order_count // inner
    period = phi_count // inner
    order_ids = lax.iota(jnp.int32, order_count)
    weights = jnp.where(order_ids == 0, 1.0, 2.0).astype(jnp.float32)
    scaled = full_coeffs * weights
    real_part = scaled[:, :sim_count].reshape(cycle_dev * sim_count, outer, inner)
    imag_part = scaled[:, sim_count:].reshape(cycle_dev * sim_count, outer, inner)
    first_cos, first_sin = phase_table(outer, period, inner, phi_count)
    high = lax.Precision.HIGHEST
    section_re = jnp.einsum("kba,bu->kau", real_part, first_cos, precision=high) - jnp.einsum(
        "kba,bu->kau", imag_part, first_sin, precision=high
    )
    section_im = jnp.einsum("kba,bu->kau", real_part, first_sin, precision=high) + jnp.einsum(
        "kba,bu->kau", imag_part, first_cos, precision=high
    )
    twist_cos, twist_sin = phase_table(inner, period, 1, phi_count)
    turned_re = section_re * twist_cos - section_im * twist_sin
    turned_im = section_re * twist_sin + section_im * twist_cos
    second_cos, second_sin = phase_table(inner, inner, period, phi_count)
    values = jnp.einsum("kau,av->kvu", turned_re, second_cos, precision=high) - jnp.einsum(
        "kau,av->kvu", turned_im, second_sin, precision=high
    )
    cycle_values = values.reshape(cycle_dev * sim_count, phi_count)
    return jnp.transpose(cycle_values.reshape(cycle_dev, sim_count, count), (1, 0, 2))


def general_body(alm, legendre, src_cycle, src_phi, off_cycle, off_phi):
    sim_count = alm.shape[1] // 2
    n_harm = lax.axis_size("harm")
    n_remap = lax.axis_size("remap")
    m_local = alm.shape[0]
    cycle_dev = src_cycle.shape[0]
    quarter = src_cycle.shape[1]
    phi_count = quarter * n_remap
    harm_index = lax.axis_index("harm")
    remap_index = lax.axis_index("remap")
    harmonic = jnp.einsum("mkl,mrl->rkm", alm, legendre, preferred_element_type=jnp.float32)
    cycle_coeffs = lax.all_to_all(harmonic, "harm", split_axis=0, concat_axis=2, tiled=True)
    group_ids = lax.iota(jnp.int32, n_remap)
    picker = jnp.where(group_ids == remap_index, 1.0, 0.0).astype(jnp.float32)
    spread = cycle_coeffs.reshape(cycle_dev, 2 * sim_count, n_harm, 1, m_local) * picker[:, None]
    full_coeffs = spread.reshape(cycle_dev, 2 * sim_count, n_harm * n_remap * m_local)
    partial_map = synthesize(full_coeffs, phi_count, phi_count, sim_count)
    unlensed = lax.psum_scatter(partial_map, "remap", scatter_dimension=2, tiled=True)
    widened = with_halo(unlensed, (("remap", 2),), DP)
    reach_devices = -(-DR // cycle_dev)
    below_parts = [
        from_behind(widened, "harm", distance) for distance in range(reach_devices, 0, -1)
    ]
    above_parts = [
        from_behind(widened, "harm", -distance) for distance in range(1, reach_devices + 1)
    ]
    window = jnp.concatenate(below_parts + [widened] + above_parts, axis=1)
    cycle_base = harm_index * cycle_dev - reach_devices * cycle_dev
    phi_base = remap_index * quarter - DP
    span = window.shape[2]
    cycle_slot = src_cycle - cycle_base
    phi_slot = (src_phi - phi_base) % phi_count
    flat_index = (cycle_slot * span + phi_slot).reshape(-1)
    flattened = window.reshape(sim_count, -1)

    def tap_values(offset):
        return jnp.take(flattened, flat_index + offset, axis=1)

    cycle_frac = (off_cycle.astype(jnp.float32) / QF).reshape(-1)
    phi_frac = (off_phi.astype(jnp.float32) / QF).reshape(-1)
    near_row = (1.0 - phi_frac) * tap_values(0) + phi_frac * tap_values(1)
    far_row = (1.0 - phi_frac) * tap_values(span) + phi_frac * tap_values(span + 1)
    mixed = (1.0 - cycle_frac) * near_row + cycle_frac * far_row
    return mixed.reshape(sim_count, cycle_dev, quarter).astype(jnp.bfloat16)


LANES = 128


def split_bf16(table):
    high = table.astype(ml_dtypes.bfloat16)
    low = (table - high.astype(np.float64)).astype(ml_dtypes.bfloat16)
    return high, low


def tables(n_harm, n_remap, phi_count):
    lane = np.arange(LANES)
    order = (lane // 8) * 4 + lane % 4
    parity = (lane // 4) % 2
    device = (np.arange(n_harm)[None, :] * n_remap + np.arange(n_remap)[:, None]).reshape(-1)
    block = (device[:, None] * 2 + np.arange(2)[None, :]).reshape(-1)
    angle = 2.0 * np.pi * ((np.arange(LANES)[:, None] * block[None, :]) % LANES) / LANES
    first = np.block([[np.cos(angle), -np.sin(angle)], [np.sin(angle), np.cos(angle)]])
    high, low = split_bf16(first)
    first_table = np.concatenate([high, high, low], axis=1).astype(np.float32)
    angle = 2.0 * np.pi * np.arange(LANES)[:, None] * order[None, :] / phi_count
    twist = np.stack([np.cos(angle), np.sin(angle)]).astype(np.float32)
    period = phi_count // LANES
    rows = np.arange(-8, period + 8) % period
    angle = 2.0 * np.pi * ((rows[:, None] * order[None, :]) % period) / period
    second = 2.0 * np.concatenate([np.cos(angle), -np.sin(angle)], axis=1)
    keep = np.concatenate([parity, parity])[None, None, :] == np.arange(2)[:, None, None]
    high, low = split_bf16(np.where(keep, second[None], 0.0))
    second_table = np.concatenate([high, low]).astype(np.float32)
    return first_table, twist, second_table


def accumulate_orders(turn, alm_ref, leg_ref, rows_ref):
    per_group, rows, depth = alm_ref.shape
    cycles = leg_ref.shape[1]
    share = LANES // rows
    coeffs = alm_ref[...].reshape(per_group * rows, depth)
    basis = leg_ref[...].reshape(per_group * cycles, depth)
    product = dot_last(basis, coeffs)
    lane = lax.broadcasted_iota(jnp.int32, (cycles, LANES), 1)
    parts = []
    for t in range(per_group // share):
        cols = slice(t * LANES, (t + 1) * LANES)
        own = jnp.zeros((cycles, LANES), jnp.float32)
        for i in range(share):
            top = (t * share + i) * cycles
            own = jnp.where(lane // rows == i, product[top : top + cycles, cols], own)
        parts.append(own)
    block = jnp.concatenate(parts, axis=0)
    height = block.shape[0]
    rows_ref[pl.ds(pl.multiple_of(turn * height, height), height), :] = block


def arrange_orders(half, rows, cycles, rows_ref, acc_ref):
    turned_rows = rows_ref[...].T
    lane = lax.broadcasted_iota(jnp.int32, (rows, LANES), 1)
    device = lax.axis_index("harm") * lax.axis_size("remap") + lax.axis_index("remap")
    first_order = jnp.logical_and(device == 0, half == 0)
    for pair in range(cycles // 2):
        total = jnp.zeros((rows, LANES), jnp.float32)
        for low in range(2):
            for i in range(LANES // rows):
                place, r = 4 * low + i, 2 * pair + low
                turned = pltpu.roll(
                    turned_rows[i * rows : (i + 1) * rows], (place - r) % LANES, axis=1
                )
                if i == 0:
                    zero = jnp.logical_and(first_order, lane == place)
                    turned = jnp.where(zero, 0.5 * turned, turned)
                total = jnp.where(lane % cycles == place, turned, total)
        acc_ref[pair * rows : (pair + 1) * rows, :] = total


def dot_last(a, b):
    return lax.dot_general(a, b, (((1,), (1,)), ((), ())), preferred_element_type=jnp.float32)


def synthesize_sim(x_ref, e, step, pairs, first, twist_ref, second, z_ref):
    blocks = x_ref.shape[0] // step
    columns = []
    for pair in range(pairs):
        columns.append(
            jnp.concatenate(
                [
                    x_ref[pl.ds((e * 2 + c) * pairs + pair, blocks, stride=step), :]
                    for c in range(2)
                ],
                axis=0,
            )
        )
    coeffs = jnp.concatenate(columns, axis=1)
    high = coeffs.astype(jnp.bfloat16)
    low = (coeffs - high.astype(jnp.float32)).astype(jnp.bfloat16)
    section = jnp.dot(
        first, jnp.concatenate([high, low, high], axis=0), preferred_element_type=jnp.float32
    )
    for pair in range(pairs):
        cols = slice(pair * LANES, (pair + 1) * LANES)
        re = section[:LANES, cols]
        im = section[LANES:, cols]
        turned = jnp.concatenate(
            [
                re * twist_ref[0] - im * twist_ref[1],
                re * twist_ref[1] + im * twist_ref[0],
            ],
            axis=1,
        )
        turned_high = turned.astype(jnp.bfloat16)
        z_ref[0, cols, :] = turned_high
        z_ref[1, cols, :] = (turned - turned_high.astype(jnp.float32)).astype(jnp.bfloat16)
    span = second.shape[0] // 2
    both = dot_last(second, z_ref[0])
    return both[:span] + both[span:] + dot_last(second[:span], z_ref[1])


def interpolate(r, cycles, per_dev, u_ref, sc, sp, oc, op, tiles):
    lane = lax.broadcasted_iota(jnp.int32, (tiles, LANES), 1)
    near_index = sp & (LANES - 1)
    far_index = (sp + 1) & (LANES - 1)
    b = op.astype(jnp.float32) * (1.0 / QF)
    a = oc.astype(jnp.float32) * (1.0 / QF)
    totals = [jnp.zeros((tiles, LANES), jnp.float32) for _ in range(per_dev)]
    for j in range(max(0, r - DR), min(cycles - 1, r + DR) + 1):
        weight = jnp.where(sc == j, 1.0 - a, jnp.where(sc == j - 1, a, 0.0))
        near_weight = weight * (1.0 - b)
        far_weight = weight * b
        for e in range(per_dev):
            left = u_ref[e, 0, j]
            right = u_ref[e, 1, j]
            near, far = (
                jnp.where(
                    lane < LANES // 2,
                    jnp.take_along_axis(left, index, axis=1, mode="promise_in_bounds"),
                    jnp.take_along_axis(right, index, axis=1, mode="promise_in_bounds"),
                )
                for index in (near_index, far_index)
            )
            totals[e] = totals[e] + near_weight * near + far_weight * far
    return totals


def to_device(src, dst, send_sem, recv_sem, axis, index):
    return pltpu.make_async_remote_copy(
        src_ref=src,
        dst_ref=dst,
        send_sem=send_sem,
        recv_sem=recv_sem,
        device_id={axis: index},
        device_id_type=pl.DeviceIdType.MESH,
    )


def sky_step(
    n_harm, n_remap, per_dev,
    alm_ref, leg_ref, sc_ref, sp_ref, oc_ref, op_ref, first_ref, twist_ref, second_ref,
    out_ref,
    rows_ref, acc_ref, pack_ref, x_ref, where_ref, z_ref, w_ref, u_ref, maps_ref, fin_ref,
    i_send, i_recv, a_send, a_recv, y_send, y_recv, s_send, s_recv, f_send, f_recv, o_send, o_recv,
):
    group = pl.program_id(0)
    groups = pl.num_programs(0)
    turns = groups // 2
    cycles = leg_ref.shape[1]
    pairs = cycles // 2
    tiles = sc_ref.shape[0]
    rows = alm_ref.shape[1]
    sims = rows // 2
    piece = per_dev * 2 * pairs
    me = lax.axis_index("harm")
    q = lax.axis_index("remap")
    across = lax.rem(q + 2, n_remap)
    sibling = q + 1 - 2 * lax.rem(q, 2)
    far = lax.rem(sibling + 2, n_remap)
    peers = [lax.rem(me + k, n_harm) for k in range(1, n_harm)]

    def slot(half, quarter, source):
        start = pl.multiple_of(((quarter * n_harm + source) * 2 + half) * piece, piece)
        return x_ref.at[pl.ds(start, piece), :]

    def packed(half, target):
        return pack_ref.at[half, pl.ds(pl.multiple_of(target * piece, piece), piece), :]

    def index_copy(source, target):
        return to_device(
            where_ref.at[source], where_ref.at[source], i_send.at[target], i_recv.at[source], "harm", target
        )

    def order_copy(half, source, target):
        return to_device(
            packed(half, target), slot(half, q, source),
            a_send.at[half, target], a_recv.at[half, source], "harm", target,
        )

    def across_copy(half, quarter, source):
        held = slot(half, quarter, source)
        return to_device(held, held, y_send.at[half, source], y_recv.at[half, source], "remap", across)

    def sibling_copy(half, quarter, source):
        held = slot(half, quarter, source)
        return to_device(held, held, s_send.at[half, source], s_recv.at[half, source], "remap", sibling)

    def forward_copy(half, quarter, source):
        held = slot(half, quarter, source)
        return to_device(held, held, f_send.at[half, source], f_recv.at[half, source], "remap", sibling)

    def map_copy(source, target):
        return to_device(
            maps_ref.at[target], fin_ref.at[source], o_send.at[target], o_recv.at[source], "harm", target
        )

    def send_orders(half):
        arrange_orders(half, rows, cycles, rows_ref, acc_ref)
        for k in range(rows):
            sim, part = k % sims, k // sims
            start = (sim // per_dev) * piece + ((sim % per_dev) * 2 + part) * pairs
            pack_ref[half, start : start + pairs, :] = acc_ref[pl.ds(k, pairs, stride=rows), :]
        for p in peers:
            order_copy(half, me, p).start()
        own = pl.multiple_of(((q * n_harm + me) * 2 + half) * piece, piece)
        mine = pl.multiple_of(me * piece, piece)
        x_ref[pl.ds(own, piece), :] = pack_ref[half, pl.ds(mine, piece), :]
        across_copy(half, q, me).start()
        sibling_copy(half, q, me).start()

    def relay_orders(half):
        for p in peers:
            order_copy(half, p, p).wait_recv()
            across_copy(half, q, p).start()
            sibling_copy(half, q, p).start()

    def forward_orders(half):
        for p in [me] + peers:
            across_copy(half, across, p).wait_recv()
            forward_copy(half, across, p).start()

    @pl.when(group == 0)
    def _():
        barrier = pltpu.get_barrier_semaphore()
        for p in peers:
            pl.semaphore_signal(
                barrier, inc=1, device_id={"harm": p}, device_id_type=pl.DeviceIdType.MESH
            )
        for p in (across, sibling):
            pl.semaphore_signal(
                barrier, inc=1, device_id={"remap": p}, device_id_type=pl.DeviceIdType.MESH
            )
        for i, ref in enumerate((sc_ref, sp_ref, oc_ref, op_ref)):
            where_ref[me, i] = ref[...]
        pl.semaphore_wait(barrier, n_harm + 1)
        for p in peers:
            index_copy(me, p).start()

    accumulate_orders(lax.rem(group, turns), alm_ref, leg_ref, rows_ref)

    @pl.when(group == turns - 1)
    def _():
        send_orders(0)

    @pl.when(group == turns + 1)
    def _():
        relay_orders(0)

    @pl.when(group == turns + 2)
    def _():
        forward_orders(0)

    @pl.when(group == groups - 1)
    def _():
        send_orders(1)
        relay_orders(1)
        forward_orders(1)
        for p in peers:
            index_copy(p, p).wait_recv()
        for half in range(2):
            for p in [me] + peers:
                sibling_copy(half, sibling, p).wait_recv()
                forward_copy(half, far, p).wait_recv()

        start = pl.multiple_of(q * tiles, tiles)
        span = tiles + 16
        second = jnp.concatenate(
            [second_ref[i, pl.ds(start, span), :] for i in range(4)], axis=0
        ).astype(jnp.bfloat16)
        first = first_ref[...].astype(jnp.bfloat16)
        lane = lax.broadcasted_iota(jnp.int32, (tiles, LANES), 1)
        for e in range(per_dev):
            w_ref[...] = synthesize_sim(x_ref, e, piece, pairs, first, twist_ref, second, z_ref)
            for j in range(cycles):
                cols = slice((j // 2) * LANES, (j // 2 + 1) * LANES)
                top = (j % 2) * span + 8
                here = w_ref[top : top + tiles, cols]
                before = w_ref[top - 1 : top - 1 + tiles, cols]
                after = w_ref[top + 1 : top + 1 + tiles, cols]
                u_ref[e, 0, j] = jnp.where(lane >= 3 * LANES // 4, before, here)
                u_ref[e, 1, j] = jnp.where(lane < LANES // 4, after, here)
        for r in range(cycles):
            totals = interpolate(
                r, cycles, per_dev, u_ref,
                where_ref[r, 0], where_ref[r, 1], where_ref[r, 2], where_ref[r, 3], tiles,
            )
            for e in range(per_dev):
                maps_ref[r, e * tiles : (e + 1) * tiles, :] = totals[e]

            @pl.when(me != r)
            def _():
                map_copy(me, r).start()

        fin_ref[me] = maps_ref[me]
        for p in peers:
            map_copy(p, p).wait_recv()
        for t in range(tiles):
            out_ref[:, t * LANES : (t + 1) * LANES] = jnp.concatenate(
                [fin_ref[h, pl.ds(t, per_dev, stride=tiles), :] for h in range(n_harm)], axis=0
            ).astype(jnp.bfloat16)
        for p in peers:
            index_copy(me, p).wait_send()
            map_copy(me, p).wait_send()
        for half in range(2):
            for p in peers:
                order_copy(half, me, p).wait_send()
            for p in [me] + peers:
                across_copy(half, q, p).wait_send()
                sibling_copy(half, q, p).wait_send()
                forward_copy(half, across, p).wait_send()


def body(alm, legendre, src_cycle, src_phi, off_cycle, off_phi):
    n_harm = lax.axis_size("harm")
    n_remap = lax.axis_size("remap")
    m_local, rows, depth = alm.shape
    sims = rows // 2
    per_dev = sims // n_harm
    cycles = legendre.shape[1]
    quarter = src_cycle.shape[1]
    tiles = quarter // LANES
    per_group = LANES // cycles
    groups = m_local // per_group
    pairs = cycles // 2
    piece = per_dev * 2 * pairs
    first_table, twist, second_table = tables(n_harm, n_remap, quarter * n_remap)
    whole = pl.BlockSpec(memory_space=pltpu.VMEM)
    single = pltpu.SemaphoreType.DMA((n_harm,))
    double = pltpu.SemaphoreType.DMA((2, n_harm))
    lensed = pl.pallas_call(
        functools.partial(sky_step, n_harm, n_remap, per_dev),
        grid=(groups,),
        in_specs=[
            pl.BlockSpec((per_group, rows, depth), lambda g: (g, 0, 0)),
            pl.BlockSpec((per_group, cycles, depth), lambda g: (g, 0, 0)),
        ]
        + [whole] * 7,
        out_specs=whole,
        out_shape=jax.ShapeDtypeStruct((sims, quarter), jnp.bfloat16),
        scratch_shapes=[
            pltpu.VMEM((LANES, LANES), jnp.float32),
            pltpu.VMEM((rows * pairs, LANES), jnp.float32),
            pltpu.VMEM((2, rows * pairs, LANES), jnp.float32),
            pltpu.VMEM((n_remap * n_harm * 2 * piece, LANES), jnp.float32),
            pltpu.VMEM((n_harm, 4, tiles, LANES), jnp.int32),
            pltpu.VMEM((2, pairs * LANES, 2 * LANES), jnp.bfloat16),
            pltpu.VMEM((2 * (tiles + 16), pairs * LANES), jnp.float32),
            pltpu.VMEM((per_dev, 2, cycles, tiles, LANES), jnp.float32),
            pltpu.VMEM((cycles, per_dev * tiles, LANES), jnp.float32),
            pltpu.VMEM((n_harm, per_dev * tiles, LANES), jnp.float32),
            single, single, double, double, double, double,
            double, double, double, double, single, single,
        ],
        compiler_params=pltpu.CompilerParams(
            collective_id=0, has_side_effects=True, vmem_limit_bytes=56 * 2**20
        ),
    )(
        alm,
        legendre,
        *(array.reshape(tiles, LANES) for array in (src_cycle, src_phi, off_cycle, off_phi)),
        jnp.asarray(first_table),
        jnp.asarray(twist),
        jnp.asarray(second_table),
    )
    return lensed.reshape(sims, 1, quarter)


def fits(mesh, alm, legendre, src_cycle):
    n_harm, n_remap = mesh.shape["harm"], mesh.shape["remap"]
    cycles = legendre.shape[1]
    sims = alm.shape[1] // 2
    phi_count = src_cycle.shape[1]
    return (
        cycles == n_harm == 8
        and alm.shape[1] == 32
        and sims % n_harm == 0
        and alm.shape[0] == LANES * n_harm * n_remap
        and phi_count == LANES * 64
        and (phi_count // n_remap) % (16 * LANES) == 0
        and (n_harm * n_remap) % 8 == 0
        and n_remap == 4
    )


def solution(mesh):
    def run(*arrays):
        chosen = body if fits(mesh, arrays[0], arrays[1], arrays[2]) else general_body
        return sharded(mesh, chosen)(*arrays)

    return run


def sharded(mesh, chosen):
    return jax.shard_map(
        chosen,
        mesh=mesh,
        in_specs=(
            P(("harm", "remap"), None, None),
            P(("harm", "remap"), None, None),
            P("harm", "remap"),
            P("harm", "remap"),
            P("harm", "remap"),
            P("harm", "remap"),
        ),
        out_specs=P(None, "harm", "remap"),
        check_vma=False,
    )
```

```python
import math

import functools

import jax
import jax.numpy as jnp
import ml_dtypes
import numpy as np
from jax import lax
from jax.experimental import pallas as pl
from jax.experimental.pallas import tpu as pltpu
from jax.sharding import PartitionSpec as P

DR = 3
DP = 8
QF = 16


def with_halo(cells, sides, width):
    for axis, dim in sides:
        count = lax.axis_size(axis)
        head = lax.slice_in_dim(cells, 0, width, axis=dim)
        tail = lax.slice_in_dim(cells, cells.shape[dim] - width, cells.shape[dim], axis=dim)
        cells = jnp.concatenate(
            [
                lax.ppermute(tail, axis, [(i, (i + 1) % count) for i in range(count)]),
                cells,
                lax.ppermute(head, axis, [((i + 1) % count, i) for i in range(count)]),
            ],
            axis=dim,
        )
    return cells


def from_behind(block, axis, distance):
    devices = range(lax.axis_size(axis))
    route = [(i - distance, i) for i in devices if i - distance in devices]
    return lax.ppermute(block, axis, route)


def phase_table(rows, cols, factor, phi_count):
    row_ids = lax.broadcasted_iota(jnp.int32, (rows, cols), 0)
    col_ids = lax.broadcasted_iota(jnp.int32, (rows, cols), 1)
    phase = factor * row_ids * col_ids % phi_count
    angles = phase.astype(jnp.float32) * (2.0 * math.pi / phi_count)
    return (jnp.cos(angles), jnp.sin(angles))


def synthesize(full_coeffs, count, phi_count, sim_count):
    cycle_dev = full_coeffs.shape[0]
    order_count = full_coeffs.shape[2]
    inner = 64
    outer = order_count // inner
    period = phi_count // inner
    order_ids = lax.iota(jnp.int32, order_count)
    weights = jnp.where(order_ids == 0, 1.0, 2.0).astype(jnp.float32)
    scaled = full_coeffs * weights
    real_part = scaled[:, :sim_count].reshape(cycle_dev * sim_count, outer, inner)
    imag_part = scaled[:, sim_count:].reshape(cycle_dev * sim_count, outer, inner)
    first_cos, first_sin = phase_table(outer, period, inner, phi_count)
    high = lax.Precision.HIGHEST
    section_re = jnp.einsum("kba,bu->kau", real_part, first_cos, precision=high) - jnp.einsum(
        "kba,bu->kau", imag_part, first_sin, precision=high
    )
    section_im = jnp.einsum("kba,bu->kau", real_part, first_sin, precision=high) + jnp.einsum(
        "kba,bu->kau", imag_part, first_cos, precision=high
    )
    twist_cos, twist_sin = phase_table(inner, period, 1, phi_count)
    turned_re = section_re * twist_cos - section_im * twist_sin
    turned_im = section_re * twist_sin + section_im * twist_cos
    second_cos, second_sin = phase_table(inner, inner, period, phi_count)
    values = jnp.einsum("kau,av->kvu", turned_re, second_cos, precision=high) - jnp.einsum(
        "kau,av->kvu", turned_im, second_sin, precision=high
    )
    cycle_values = values.reshape(cycle_dev * sim_count, phi_count)
    return jnp.transpose(cycle_values.reshape(cycle_dev, sim_count, count), (1, 0, 2))


def general_body(alm, legendre, src_cycle, src_phi, off_cycle, off_phi):
    sim_count = alm.shape[1] // 2
    n_harm = lax.axis_size("harm")
    n_remap = lax.axis_size("remap")
    m_local = alm.shape[0]
    cycle_dev = src_cycle.shape[0]
    quarter = src_cycle.shape[1]
    phi_count = quarter * n_remap
    harm_index = lax.axis_index("harm")
    remap_index = lax.axis_index("remap")
    harmonic = jnp.einsum("mkl,mrl->rkm", alm, legendre, preferred_element_type=jnp.float32)
    cycle_coeffs = lax.all_to_all(harmonic, "harm", split_axis=0, concat_axis=2, tiled=True)
    group_ids = lax.iota(jnp.int32, n_remap)
    picker = jnp.where(group_ids == remap_index, 1.0, 0.0).astype(jnp.float32)
    spread = cycle_coeffs.reshape(cycle_dev, 2 * sim_count, n_harm, 1, m_local) * picker[:, None]
    full_coeffs = spread.reshape(cycle_dev, 2 * sim_count, n_harm * n_remap * m_local)
    partial_map = synthesize(full_coeffs, phi_count, phi_count, sim_count)
    unlensed = lax.psum_scatter(partial_map, "remap", scatter_dimension=2, tiled=True)
    widened = with_halo(unlensed, (("remap", 2),), DP)
    reach_devices = -(-DR // cycle_dev)
    below_parts = [
        from_behind(widened, "harm", distance) for distance in range(reach_devices, 0, -1)
    ]
    above_parts = [
        from_behind(widened, "harm", -distance) for distance in range(1, reach_devices + 1)
    ]
    window = jnp.concatenate(below_parts + [widened] + above_parts, axis=1)
    cycle_base = harm_index * cycle_dev - reach_devices * cycle_dev
    phi_base = remap_index * quarter - DP
    span = window.shape[2]
    cycle_slot = src_cycle - cycle_base
    phi_slot = (src_phi - phi_base) % phi_count
    flat_index = (cycle_slot * span + phi_slot).reshape(-1)
    flattened = window.reshape(sim_count, -1)

    def tap_values(offset):
        return jnp.take(flattened, flat_index + offset, axis=1)

    cycle_frac = (off_cycle.astype(jnp.float32) / QF).reshape(-1)
    phi_frac = (off_phi.astype(jnp.float32) / QF).reshape(-1)
    near_row = (1.0 - phi_frac) * tap_values(0) + phi_frac * tap_values(1)
    far_row = (1.0 - phi_frac) * tap_values(span) + phi_frac * tap_values(span + 1)
    mixed = (1.0 - cycle_frac) * near_row + cycle_frac * far_row
    return mixed.reshape(sim_count, cycle_dev, quarter).astype(jnp.bfloat16)


LANES = 128


def split_bf16(table):
    high = table.astype(ml_dtypes.bfloat16)
    low = (table - high.astype(np.float64)).astype(ml_dtypes.bfloat16)
    return high, low


def tables(n_harm, n_remap, phi_count):
    lane = np.arange(LANES)
    order = lane % (LANES // 2)
    parity = lane // (LANES // 2)
    device = (np.arange(n_harm)[None, :] * n_remap + np.arange(n_remap)[:, None]).reshape(-1)
    block = (device[:, None] * 2 + np.arange(2)[None, :]).reshape(-1)
    angle = 2.0 * np.pi * ((np.arange(LANES)[:, None] * block[None, :]) % LANES) / LANES
    first = np.block([[np.cos(angle), -np.sin(angle)], [np.sin(angle), np.cos(angle)]])
    high, low = split_bf16(first)
    first_table = np.concatenate([high, high, low], axis=1).astype(np.float32)
    angle = 2.0 * np.pi * np.arange(LANES)[:, None] * order[None, :] / phi_count
    twist = np.stack([np.cos(angle), np.sin(angle)]).astype(np.float32)
    period = phi_count // LANES
    rows = np.arange(-8, period + 8) % period
    angle = 2.0 * np.pi * ((rows[:, None] * order[None, :]) % period) / period
    second = 2.0 * np.concatenate([np.cos(angle), -np.sin(angle)], axis=1)
    keep = np.concatenate([parity, parity])[None, None, :] == np.arange(2)[:, None, None]
    high, low = split_bf16(np.where(keep, second[None], 0.0))
    second_table = np.concatenate([high, low]).astype(np.float32)
    return first_table, twist, second_table


def dot_last(a, b):
    return lax.dot_general(a, b, (((1,), (1,)), ((), ())), preferred_element_type=jnp.float32)


def synthesize_sim(x_ref, e, step, pairs, first, twist_ref, second, z_ref):
    blocks = x_ref.shape[0] // step
    columns = []
    for pair in range(pairs):
        columns.append(
            jnp.concatenate(
                [
                    x_ref[pl.ds((e * 2 + c) * pairs + pair, blocks, stride=step), :]
                    for c in range(2)
                ],
                axis=0,
            )
        )
    coeffs = jnp.concatenate(columns, axis=1)
    high = coeffs.astype(jnp.bfloat16)
    low = (coeffs - high.astype(jnp.float32)).astype(jnp.bfloat16)
    section = jnp.dot(
        first, jnp.concatenate([high, low, high], axis=0), preferred_element_type=jnp.float32
    )
    for pair in range(pairs):
        cols = slice(pair * LANES, (pair + 1) * LANES)
        re = section[:LANES, cols]
        im = section[LANES:, cols]
        turned = jnp.concatenate(
            [
                re * twist_ref[0] - im * twist_ref[1],
                re * twist_ref[1] + im * twist_ref[0],
            ],
            axis=1,
        )
        turned_high = turned.astype(jnp.bfloat16)
        z_ref[0, cols, :] = turned_high
        z_ref[1, cols, :] = (turned - turned_high.astype(jnp.float32)).astype(jnp.bfloat16)
    span = second.shape[0] // 2
    both = dot_last(second, z_ref[0])
    return both[:span] + both[span:] + dot_last(second[:span], z_ref[1])


def interpolate(r, cycles, e, u_ref, sc, sp, oc, op, tiles):
    lane = lax.broadcasted_iota(jnp.int32, (tiles, LANES), 1)
    near_index = sp & (LANES - 1)
    far_index = (sp + 1) & (LANES - 1)
    b = op.astype(jnp.float32) * (1.0 / QF)
    a = oc.astype(jnp.float32) * (1.0 / QF)
    total = jnp.zeros((tiles, LANES), jnp.float32)
    for j in range(max(0, r - DR), min(cycles - 1, r + DR) + 1):
        weight = jnp.where(sc == j, 1.0 - a, jnp.where(sc == j - 1, a, 0.0))
        left = u_ref[e, 0, j]
        right = u_ref[e, 1, j]
        near, far = (
            jnp.where(
                lane < LANES // 2,
                jnp.take_along_axis(left, index, axis=1, mode="promise_in_bounds"),
                jnp.take_along_axis(right, index, axis=1, mode="promise_in_bounds"),
            )
            for index in (near_index, far_index)
        )
        total = total + weight * ((1.0 - b) * near + b * far)
    return total


def to_device(src, dst, send_sem, recv_sem, axis, index):
    return pltpu.make_async_remote_copy(
        src_ref=src,
        dst_ref=dst,
        send_sem=send_sem,
        recv_sem=recv_sem,
        device_id={axis: index},
        device_id_type=pl.DeviceIdType.MESH,
    )


def sky_step(
    n_harm, n_remap, per_dev,
    sums_ref, sc_ref, sp_ref, oc_ref, op_ref, first_ref, twist_ref, second_ref,
    out_ref,
    half_ref, pack_ref, x_ref, where_ref, z_ref, w_ref, u_ref, maps_ref, fin_ref,
    i_send, i_recv, a_send, a_recv, y_send, y_recv, s_send, s_recv, f_send, f_recv, o_send, o_recv,
):
    cycles, rows, _ = sums_ref.shape
    pairs = cycles // 2
    tiles = sc_ref.shape[0]
    sims = rows // 2
    half_piece = per_dev * 2 * pairs
    piece = 2 * half_piece
    me = lax.axis_index("harm")
    q = lax.axis_index("remap")
    across = lax.rem(q + 2, n_remap)
    sibling = q + 1 - 2 * lax.rem(q, 2)
    far = lax.rem(sibling + 2, n_remap)
    peers = [lax.rem(me + k, n_harm) for k in range(1, n_harm)]

    def slot(quarter, source):
        start = pl.multiple_of((quarter * n_harm + source) * piece, piece)
        return x_ref.at[pl.ds(start, piece), :]

    def packed(target):
        return pack_ref.at[pl.ds(pl.multiple_of(target * piece, piece), piece), :]

    def order_copy(source, target):
        return to_device(
            packed(target), slot(q, source), a_send.at[target], a_recv.at[source], "harm", target
        )

    def across_copy(quarter, source):
        held = slot(quarter, source)
        return to_device(held, held, y_send.at[source], y_recv.at[source], "remap", across)

    def sibling_copy(quarter, source):
        held = slot(quarter, source)
        return to_device(held, held, s_send.at[source], s_recv.at[source], "remap", sibling)

    def forward_copy(quarter, source):
        held = slot(quarter, source)
        return to_device(held, held, f_send.at[source], f_recv.at[source], "remap", sibling)

    def map_copy(e, source, target):
        part = pl.ds(e * tiles, tiles)
        return to_device(
            maps_ref.at[target, part], fin_ref.at[source, part],
            o_send.at[e, target], o_recv.at[e, source], "harm", target,
        )

    def index_copy(source, target):
        held = where_ref.at[source]
        return to_device(held, held, i_send.at[target], i_recv.at[source], "harm", target)

    barrier = pltpu.get_barrier_semaphore()
    for p in peers:
        pl.semaphore_signal(
            barrier, inc=1, device_id={"harm": p}, device_id_type=pl.DeviceIdType.MESH
        )
    for p in (across, sibling):
        pl.semaphore_signal(
            barrier, inc=1, device_id={"remap": p}, device_id_type=pl.DeviceIdType.MESH
        )
    for i, ref in enumerate((sc_ref, sp_ref, oc_ref, op_ref)):
        where_ref[me, i] = ref[...]
    device = me * n_remap + q
    row_lane = lax.broadcasted_iota(jnp.int32, (rows, LANES), 1)
    for pair in range(pairs):
        even, odd = sums_ref[2 * pair], sums_ref[2 * pair + 1]
        zero_order = jnp.logical_and(device == 0, row_lane == 0)
        even = jnp.where(zero_order, 0.5 * even, even)
        odd = jnp.where(zero_order, 0.5 * odd, odd)
        half_ref[pair * rows : (pair + 1) * rows, :] = jnp.where(
            row_lane < LANES // 2, even, pltpu.roll(odd, LANES // 2, axis=1)
        )
        half_ref[(pairs + pair) * rows : (pairs + pair + 1) * rows, :] = jnp.where(
            row_lane < LANES // 2, pltpu.roll(even, LANES // 2, axis=1), odd
        )
    for half in range(2):
        for k in range(rows):
            sim, part = k % sims, k // sims
            start = (sim // per_dev) * piece + half * half_piece
            start += ((sim % per_dev) * 2 + part) * pairs
            pack_ref[start : start + pairs, :] = half_ref[
                pl.ds(half * pairs * rows + k, pairs, stride=rows), :
            ]
    pl.semaphore_wait(barrier, n_harm + 1)
    for p in peers:
        order_copy(me, p).start()
    own = pl.multiple_of((q * n_harm + me) * piece, piece)
    x_ref[pl.ds(own, piece), :] = pack_ref[pl.ds(pl.multiple_of(me * piece, piece), piece), :]
    across_copy(q, me).start()
    sibling_copy(q, me).start()
    for p in peers:
        index_copy(me, p).start()
    for p in peers:
        order_copy(p, p).wait_recv()
        across_copy(q, p).start()
        sibling_copy(q, p).start()
    for p in [me] + peers:
        across_copy(across, p).wait_recv()
        forward_copy(across, p).start()
    for p in [me] + peers:
        sibling_copy(sibling, p).wait_recv()
        forward_copy(far, p).wait_recv()

    start = pl.multiple_of(q * tiles, tiles)
    span = tiles + 16
    second = jnp.concatenate(
        [second_ref[i, pl.ds(start, span), :] for i in range(4)], axis=0
    ).astype(jnp.bfloat16)
    first = first_ref[...].astype(jnp.bfloat16)
    lane = lax.broadcasted_iota(jnp.int32, (tiles, LANES), 1)
    for e in range(per_dev):
        w_ref[...] = synthesize_sim(x_ref, e, half_piece, pairs, first, twist_ref, second, z_ref)
        for j in range(cycles):
            cols = slice((j // 2) * LANES, (j // 2 + 1) * LANES)
            top = (j % 2) * span + 8
            here = w_ref[top : top + tiles, cols]
            before = w_ref[top - 1 : top - 1 + tiles, cols]
            after = w_ref[top + 1 : top + 1 + tiles, cols]
            u_ref[e, 0, j] = jnp.where(lane >= 3 * LANES // 4, before, here)
            u_ref[e, 1, j] = jnp.where(lane < LANES // 4, after, here)
        if e == 0:
            for p in peers:
                index_copy(p, p).wait_recv()
        for r in range(cycles):
            maps_ref[r, e * tiles : (e + 1) * tiles, :] = interpolate(
                r, cycles, e, u_ref,
                where_ref[r, 0], where_ref[r, 1], where_ref[r, 2], where_ref[r, 3], tiles,
            )

            @pl.when(me != r)
            def _(e=e, r=r):
                map_copy(e, me, r).start()

    fin_ref[me] = maps_ref[me]
    for e in range(per_dev):
        for p in peers:
            map_copy(e, p, p).wait_recv()
    for t in range(tiles):
        out_ref[:, t * LANES : (t + 1) * LANES] = jnp.concatenate(
            [fin_ref[h, pl.ds(t, per_dev, stride=tiles), :] for h in range(n_harm)], axis=0
        ).astype(jnp.bfloat16)
    for p in peers:
        index_copy(me, p).wait_send()
        order_copy(me, p).wait_send()
        for e in range(per_dev):
            map_copy(e, me, p).wait_send()
    for p in [me] + peers:
        across_copy(q, p).wait_send()
        sibling_copy(q, p).wait_send()
        forward_copy(across, p).wait_send()


def body(alm, legendre, src_cycle, src_phi, off_cycle, off_phi):
    n_harm = lax.axis_size("harm")
    n_remap = lax.axis_size("remap")
    rows = alm.shape[1]
    sims = rows // 2
    per_dev = sims // n_harm
    cycles = legendre.shape[1]
    quarter = src_cycle.shape[1]
    tiles = quarter // LANES
    pairs = cycles // 2
    piece = per_dev * 4 * pairs
    first_table, twist, second_table = tables(n_harm, n_remap, quarter * n_remap)
    where = [array.reshape(tiles, LANES) for array in (src_cycle, src_phi, off_cycle, off_phi)]
    sums = jnp.einsum("mkl,mrl->rkm", alm, legendre, preferred_element_type=jnp.float32)
    whole = pl.BlockSpec(memory_space=pltpu.VMEM)
    lensed = pl.pallas_call(
        functools.partial(sky_step, n_harm, n_remap, per_dev),
        in_specs=[whole] * 8,
        out_specs=whole,
        out_shape=jax.ShapeDtypeStruct((sims, quarter), jnp.bfloat16),
        scratch_shapes=[
            pltpu.VMEM((rows * 2 * pairs, LANES), jnp.float32),
            pltpu.VMEM((rows * 2 * pairs, LANES), jnp.float32),
            pltpu.VMEM((n_remap * n_harm * piece, LANES), jnp.float32),
            pltpu.VMEM((n_harm, 4, tiles, LANES), jnp.int32),
            pltpu.VMEM((2, pairs * LANES, 2 * LANES), jnp.bfloat16),
            pltpu.VMEM((2 * (tiles + 16), pairs * LANES), jnp.float32),
            pltpu.VMEM((per_dev, 2, cycles, tiles, LANES), jnp.float32),
            pltpu.VMEM((cycles, per_dev * tiles, LANES), jnp.float32),
            pltpu.VMEM((n_harm, per_dev * tiles, LANES), jnp.float32),
        ]
        + [pltpu.SemaphoreType.DMA((n_harm,)) for _ in range(10)]
        + [pltpu.SemaphoreType.DMA((per_dev, n_harm)) for _ in range(2)],
        compiler_params=pltpu.CompilerParams(
            collective_id=0, has_side_effects=True, vmem_limit_bytes=16 * 2**20
        ),
    )(
        sums,
        *where,
        jnp.asarray(first_table),
        jnp.asarray(twist),
        jnp.asarray(second_table),
    )
    return lensed.reshape(sims, 1, quarter)


def fits(mesh, alm, legendre, src_cycle):
    n_harm, n_remap = mesh.shape["harm"], mesh.shape["remap"]
    cycles = legendre.shape[1]
    sims = alm.shape[1] // 2
    phi_count = src_cycle.shape[1]
    return (
        cycles == n_harm == 8
        and sims % n_harm == 0
        and alm.shape[0] == LANES * n_harm * n_remap
        and phi_count == LANES * 64
        and (phi_count // n_remap) % (16 * LANES) == 0
        and (n_harm * n_remap) % 8 == 0
        and n_remap == 4
    )


def solution(mesh):
    def run(*arrays):
        chosen = body if fits(mesh, arrays[0], arrays[1], arrays[2]) else general_body
        return sharded(mesh, chosen)(*arrays)

    return run


def sharded(mesh, chosen):
    return jax.shard_map(
        chosen,
        mesh=mesh,
        in_specs=(
            P(("harm", "remap"), None, None),
            P(("harm", "remap"), None, None),
            P("harm", "remap"),
            P("harm", "remap"),
            P("harm", "remap"),
            P("harm", "remap"),
        ),
        out_specs=P(None, "harm", "remap"),
        check_vma=False,
    )
```

```python
import math

import functools

import jax
import jax.numpy as jnp
import ml_dtypes
import numpy as np
from jax import lax
from jax.experimental import pallas as pl
from jax.experimental.pallas import tpu as pltpu
from jax.sharding import PartitionSpec as P

DR = 3
DP = 8
QF = 16


def with_halo(cells, sides, width):
    for axis, dim in sides:
        count = lax.axis_size(axis)
        head = lax.slice_in_dim(cells, 0, width, axis=dim)
        tail = lax.slice_in_dim(cells, cells.shape[dim] - width, cells.shape[dim], axis=dim)
        cells = jnp.concatenate(
            [
                lax.ppermute(tail, axis, [(i, (i + 1) % count) for i in range(count)]),
                cells,
                lax.ppermute(head, axis, [((i + 1) % count, i) for i in range(count)]),
            ],
            axis=dim,
        )
    return cells


def from_behind(block, axis, distance):
    devices = range(lax.axis_size(axis))
    route = [(i - distance, i) for i in devices if i - distance in devices]
    return lax.ppermute(block, axis, route)


def phase_table(rows, cols, factor, phi_count):
    row_ids = lax.broadcasted_iota(jnp.int32, (rows, cols), 0)
    col_ids = lax.broadcasted_iota(jnp.int32, (rows, cols), 1)
    phase = factor * row_ids * col_ids % phi_count
    angles = phase.astype(jnp.float32) * (2.0 * math.pi / phi_count)
    return (jnp.cos(angles), jnp.sin(angles))


def synthesize(full_coeffs, count, phi_count, sim_count):
    cycle_dev = full_coeffs.shape[0]
    order_count = full_coeffs.shape[2]
    inner = 64
    outer = order_count // inner
    period = phi_count // inner
    order_ids = lax.iota(jnp.int32, order_count)
    weights = jnp.where(order_ids == 0, 1.0, 2.0).astype(jnp.float32)
    scaled = full_coeffs * weights
    real_part = scaled[:, :sim_count].reshape(cycle_dev * sim_count, outer, inner)
    imag_part = scaled[:, sim_count:].reshape(cycle_dev * sim_count, outer, inner)
    first_cos, first_sin = phase_table(outer, period, inner, phi_count)
    high = lax.Precision.HIGHEST
    section_re = jnp.einsum("kba,bu->kau", real_part, first_cos, precision=high) - jnp.einsum(
        "kba,bu->kau", imag_part, first_sin, precision=high
    )
    section_im = jnp.einsum("kba,bu->kau", real_part, first_sin, precision=high) + jnp.einsum(
        "kba,bu->kau", imag_part, first_cos, precision=high
    )
    twist_cos, twist_sin = phase_table(inner, period, 1, phi_count)
    turned_re = section_re * twist_cos - section_im * twist_sin
    turned_im = section_re * twist_sin + section_im * twist_cos
    second_cos, second_sin = phase_table(inner, inner, period, phi_count)
    values = jnp.einsum("kau,av->kvu", turned_re, second_cos, precision=high) - jnp.einsum(
        "kau,av->kvu", turned_im, second_sin, precision=high
    )
    cycle_values = values.reshape(cycle_dev * sim_count, phi_count)
    return jnp.transpose(cycle_values.reshape(cycle_dev, sim_count, count), (1, 0, 2))


def general_body(alm, legendre, src_cycle, src_phi, off_cycle, off_phi):
    sim_count = alm.shape[1] // 2
    n_harm = lax.axis_size("harm")
    n_remap = lax.axis_size("remap")
    m_local = alm.shape[0]
    cycle_dev = src_cycle.shape[0]
    quarter = src_cycle.shape[1]
    phi_count = quarter * n_remap
    harm_index = lax.axis_index("harm")
    remap_index = lax.axis_index("remap")
    harmonic = jnp.einsum("mkl,mrl->rkm", alm, legendre, preferred_element_type=jnp.float32)
    cycle_coeffs = lax.all_to_all(harmonic, "harm", split_axis=0, concat_axis=2, tiled=True)
    group_ids = lax.iota(jnp.int32, n_remap)
    picker = jnp.where(group_ids == remap_index, 1.0, 0.0).astype(jnp.float32)
    spread = cycle_coeffs.reshape(cycle_dev, 2 * sim_count, n_harm, 1, m_local) * picker[:, None]
    full_coeffs = spread.reshape(cycle_dev, 2 * sim_count, n_harm * n_remap * m_local)
    partial_map = synthesize(full_coeffs, phi_count, phi_count, sim_count)
    unlensed = lax.psum_scatter(partial_map, "remap", scatter_dimension=2, tiled=True)
    widened = with_halo(unlensed, (("remap", 2),), DP)
    reach_devices = -(-DR // cycle_dev)
    below_parts = [
        from_behind(widened, "harm", distance) for distance in range(reach_devices, 0, -1)
    ]
    above_parts = [
        from_behind(widened, "harm", -distance) for distance in range(1, reach_devices + 1)
    ]
    window = jnp.concatenate(below_parts + [widened] + above_parts, axis=1)
    cycle_base = harm_index * cycle_dev - reach_devices * cycle_dev
    phi_base = remap_index * quarter - DP
    span = window.shape[2]
    cycle_slot = src_cycle - cycle_base
    phi_slot = (src_phi - phi_base) % phi_count
    flat_index = (cycle_slot * span + phi_slot).reshape(-1)
    flattened = window.reshape(sim_count, -1)

    def tap_values(offset):
        return jnp.take(flattened, flat_index + offset, axis=1)

    cycle_frac = (off_cycle.astype(jnp.float32) / QF).reshape(-1)
    phi_frac = (off_phi.astype(jnp.float32) / QF).reshape(-1)
    near_row = (1.0 - phi_frac) * tap_values(0) + phi_frac * tap_values(1)
    far_row = (1.0 - phi_frac) * tap_values(span) + phi_frac * tap_values(span + 1)
    mixed = (1.0 - cycle_frac) * near_row + cycle_frac * far_row
    return mixed.reshape(sim_count, cycle_dev, quarter).astype(jnp.bfloat16)


LANES = 128


def split_bf16(table):
    high = table.astype(ml_dtypes.bfloat16)
    low = (table - high.astype(np.float64)).astype(ml_dtypes.bfloat16)
    return high, low


def tables(n_harm, n_remap, phi_count):
    groups = n_harm * n_remap
    period = phi_count // LANES
    order = (np.arange(n_harm)[None, :] * n_remap + np.arange(n_remap)[:, None]).reshape(-1)
    angle = 2.0 * np.pi * ((np.arange(period)[:, None] * order[None, :]) % period) / period
    first = np.block([[np.cos(angle), -np.sin(angle)], [np.sin(angle), np.cos(angle)]])
    high, low = split_bf16(first)
    first_table = np.concatenate([high, high, low], axis=1)
    angle = 2.0 * np.pi * np.arange(LANES)[:, None] * np.arange(LANES)[None, :] / phi_count
    twist = np.stack([np.cos(angle), np.sin(angle)]).astype(np.float32)
    blocks = np.arange(-8, period + 8) % period
    angle = 2.0 * np.pi * ((blocks[:, None] * np.arange(LANES)[None, :]) % period) / period
    high, low = split_bf16(2.0 * np.concatenate([np.cos(angle), -np.sin(angle)], axis=1))
    second_table = np.stack([high, low])
    return first_table, twist, second_table


def accumulate_orders(group, alm_ref, leg_ref, acc_ref):
    per_group, _, rows, depth = alm_ref.shape
    cycles = leg_ref.shape[2]
    coeffs = alm_ref[...].reshape(per_group * rows, depth)
    basis = leg_ref[...].reshape(per_group * cycles, depth)
    product = lax.dot_general(
        coeffs, basis, (((1,), (1,)), ((), ())), preferred_element_type=jnp.float32
    )
    lane = lax.broadcasted_iota(jnp.int32, (rows, LANES), 1)
    own = jnp.zeros((rows, LANES), jnp.float32)
    for i in range(per_group):
        own = jnp.where(lane // cycles == i, product[i * rows : (i + 1) * rows], own)
    device = lax.axis_index("harm") * lax.axis_size("remap") + lax.axis_index("remap")
    first_order = jnp.logical_and(device == 0, group == 0)
    for r in range(cycles):
        turned = pltpu.roll(own, lax.rem(group - r + LANES, LANES), axis=1)
        turned = jnp.where(jnp.logical_and(first_order, lane == 0), 0.5 * turned, turned)
        held = acc_ref[r * rows : (r + 1) * rows, :]
        acc_ref[r * rows : (r + 1) * rows, :] = jnp.where(lane % cycles == group, turned, held)


def dot_last(a, b):
    return lax.dot_general(a, b, (((1,), (1,)), ((), ())), preferred_element_type=jnp.float32)


def synthesize_sim(x_ref, e, per_dev, cycles, first_ref, twist_ref, second, z_ref):
    step = per_dev * 2 * cycles
    groups = x_ref.shape[0] // step
    half = first_ref.shape[0] // 2
    columns = []
    for r in range(cycles):
        columns.append(
            jnp.concatenate(
                [
                    x_ref[pl.ds((e * 2 + c) * cycles + r, groups, stride=step), :]
                    for c in range(2)
                ],
                axis=0,
            )
        )
    coeffs = jnp.concatenate(columns, axis=1)
    high = coeffs.astype(jnp.bfloat16)
    low = (coeffs - high.astype(jnp.float32)).astype(jnp.bfloat16)
    section = jnp.dot(
        first_ref[...].astype(jnp.bfloat16),
        jnp.concatenate([high, low, high], axis=0),
        preferred_element_type=jnp.float32,
    )
    for r in range(cycles):
        re = section[:half, r * LANES : (r + 1) * LANES]
        im = section[half:, r * LANES : (r + 1) * LANES]
        re = jnp.concatenate([re] * (LANES // half), axis=0)
        im = jnp.concatenate([im] * (LANES // half), axis=0)
        turned = jnp.concatenate(
            [
                re * twist_ref[0] - im * twist_ref[1],
                re * twist_ref[1] + im * twist_ref[0],
            ],
            axis=1,
        )
        turned_high = turned.astype(jnp.bfloat16)
        z_ref[0, r * LANES : (r + 1) * LANES, :] = turned_high
        z_ref[1, r * LANES : (r + 1) * LANES, :] = (
            turned - turned_high.astype(jnp.float32)
        ).astype(jnp.bfloat16)
    span = second.shape[0] // 2
    both = dot_last(second, z_ref[0])
    return both[:span] + both[span:] + dot_last(second[:span], z_ref[1])


def interpolate(e, r, cycles, u_ref, sc, sp, oc, op, tiles):
    lane = lax.broadcasted_iota(jnp.int32, (tiles, LANES), 1)
    near_index = sp & (LANES - 1)
    far_index = (sp + 1) & (LANES - 1)
    b = op.astype(jnp.float32) * (1.0 / QF)
    a = oc.astype(jnp.float32) * (1.0 / QF)
    total = jnp.zeros((tiles, LANES), jnp.float32)
    for j in range(max(0, r - DR), min(cycles - 1, r + DR) + 1):
        left = u_ref[e, 0, j]
        right = u_ref[e, 1, j]

        def tap(index):
            return jnp.where(
                lane < LANES // 2,
                jnp.take_along_axis(left, index, axis=1, mode="promise_in_bounds"),
                jnp.take_along_axis(right, index, axis=1, mode="promise_in_bounds"),
            )

        weight = jnp.where(sc == j, 1.0 - a, 0.0) + jnp.where(sc == j - 1, a, 0.0)
        total = total + weight * ((1.0 - b) * tap(near_index) + b * tap(far_index))
    return total


def to_device(src, dst, send_sem, recv_sem, axis, index):
    return pltpu.make_async_remote_copy(
        src_ref=src,
        dst_ref=dst,
        send_sem=send_sem,
        recv_sem=recv_sem,
        device_id={axis: index},
        device_id_type=pl.DeviceIdType.MESH,
    )


def sky_step(
    n_harm, n_remap, per_dev,
    alm_ref, leg_ref, sc_ref, sp_ref, oc_ref, op_ref, first_ref, twist_ref, second_ref,
    out_ref,
    acc_ref, pack_ref, x_ref, where_ref, z_ref, w_ref, u_ref, maps_ref, fin_ref,
    i_send, i_recv, a_send, a_recv, y_send, y_recv, s_send, s_recv, f_send, f_recv, o_send, o_recv,
):
    group = pl.program_id(0)
    cycles = leg_ref.shape[2]
    tiles = sc_ref.shape[0]
    rows = alm_ref.shape[2]
    piece = per_dev * 2 * cycles
    me = lax.axis_index("harm")
    q = lax.axis_index("remap")
    across = lax.rem(q + 2, n_remap)
    sibling = q + 1 - 2 * lax.rem(q, 2)
    far = lax.rem(sibling + 2, n_remap)
    peers = [lax.rem(me + k, n_harm) for k in range(1, n_harm)]

    def slot(quarter, source):
        start = pl.multiple_of((quarter * n_harm + source) * piece, piece)
        return x_ref.at[pl.ds(start, piece), :]

    def packed(target):
        return pack_ref.at[pl.ds(pl.multiple_of(target * piece, piece), piece), :]

    def index_copy(source, target):
        return to_device(
            where_ref.at[source], where_ref.at[source], i_send.at[target], i_recv.at[source], "harm", target
        )

    def order_copy(source, target):
        return to_device(
            packed(target), slot(q, source), a_send.at[target], a_recv.at[source], "harm", target
        )

    def across_copy(quarter, source):
        return to_device(
            slot(quarter, source), slot(quarter, source), y_send.at[source], y_recv.at[source], "remap", across
        )

    def sibling_copy(quarter, source):
        return to_device(
            slot(quarter, source), slot(quarter, source), s_send.at[source], s_recv.at[source], "remap", sibling
        )

    def forward_copy(quarter, source):
        return to_device(
            slot(quarter, source), slot(quarter, source), f_send.at[source], f_recv.at[source], "remap", sibling
        )

    def map_copy(source, target):
        return to_device(
            maps_ref.at[target], fin_ref.at[source], o_send.at[target], o_recv.at[source], "harm", target
        )

    @pl.when(group == 0)
    def _():
        barrier = pltpu.get_barrier_semaphore()
        for p in peers:
            pl.semaphore_signal(
                barrier, inc=1, device_id={"harm": p}, device_id_type=pl.DeviceIdType.MESH
            )
        for p in (across, sibling):
            pl.semaphore_signal(
                barrier, inc=1, device_id={"remap": p}, device_id_type=pl.DeviceIdType.MESH
            )
        for i, ref in enumerate((sc_ref, sp_ref, oc_ref, op_ref)):
            where_ref[me, i] = ref[...]

    accumulate_orders(group, alm_ref, leg_ref, acc_ref)

    @pl.when(group == 0)
    def _():
        pl.semaphore_wait(pltpu.get_barrier_semaphore(), n_harm + 1)
        for p in peers:
            index_copy(me, p).start()

    @pl.when(group == pl.num_programs(0) - 1)
    def _():
        sims = rows // 2
        for k in range(rows):
            sim, part = k % sims, k // sims
            start = (sim // per_dev) * piece + (sim % per_dev) * 2 * cycles + part * cycles
            pack_ref[start : start + cycles, :] = acc_ref[pl.ds(k, cycles, stride=rows), :]
        for p in reversed(peers):
            order_copy(me, p).start()
        own = pl.multiple_of((q * n_harm + me) * piece, piece)
        x_ref[pl.ds(own, piece), :] = pack_ref[pl.ds(pl.multiple_of(me * piece, piece), piece), :]
        across_copy(q, me).start()
        sibling_copy(q, me).start()
        for p in peers:
            order_copy(p, p).wait_recv()
            across_copy(q, p).start()
            sibling_copy(q, p).start()
        for p in [me] + peers:
            across_copy(across, p).wait_recv()
            forward_copy(across, p).start()
        for p in peers:
            index_copy(p, p).wait_recv()
        for p in [me] + peers:
            sibling_copy(sibling, p).wait_recv()
        for p in [me] + peers:
            forward_copy(far, p).wait_recv()

        start = pl.multiple_of(q * tiles, tiles)
        span = tiles + 16
        second = jnp.concatenate(
            [second_ref[0, pl.ds(start, span), :], second_ref[1, pl.ds(start, span), :]], axis=0
        ).astype(jnp.bfloat16)
        lane = lax.broadcasted_iota(jnp.int32, (tiles, LANES), 1)
        for e in range(per_dev):
            w_ref[...] = synthesize_sim(
                x_ref, e, per_dev, cycles, first_ref, twist_ref, second, z_ref
            )
            for j in range(cycles):
                cols = slice(j * LANES, (j + 1) * LANES)
                here = w_ref[8 : 8 + tiles, cols]
                u_ref[e, 0, j] = jnp.where(lane >= 3 * LANES // 4, w_ref[7 : 7 + tiles, cols], here)
                u_ref[e, 1, j] = jnp.where(lane < LANES // 4, w_ref[9 : 9 + tiles, cols], here)
        for r in range(cycles):
            for e in range(per_dev):
                maps_ref[r, e * tiles : (e + 1) * tiles, :] = interpolate(
                    e, r, cycles, u_ref,
                    where_ref[r, 0], where_ref[r, 1], where_ref[r, 2], where_ref[r, 3], tiles,
                )

            @pl.when(me != r)
            def _():
                map_copy(me, r).start()

        fin_ref[me] = maps_ref[me]
        for p in peers:
            map_copy(p, p).wait_recv()
        for t in range(tiles):
            out_ref[:, t * LANES : (t + 1) * LANES] = jnp.concatenate(
                [fin_ref[h, pl.ds(t, per_dev, stride=tiles), :] for h in range(n_harm)], axis=0
            ).astype(jnp.bfloat16)
        for p in peers:
            index_copy(me, p).wait_send()
            order_copy(me, p).wait_send()
            map_copy(me, p).wait_send()
        for p in [me] + peers:
            across_copy(q, p).wait_send()
            sibling_copy(q, p).wait_send()
            forward_copy(across, p).wait_send()


def body(alm, legendre, src_cycle, src_phi, off_cycle, off_phi):
    n_harm = lax.axis_size("harm")
    n_remap = lax.axis_size("remap")
    m_local, rows, depth = alm.shape
    sims = rows // 2
    per_dev = sims // n_harm
    cycles = legendre.shape[1]
    quarter = src_cycle.shape[1]
    tiles = quarter // LANES
    per_group = LANES // cycles
    groups = m_local // per_group
    piece = per_dev * 2 * cycles
    first_table, twist, second_table = tables(n_harm, n_remap, quarter * n_remap)
    whole = pl.BlockSpec(memory_space=pltpu.VMEM)
    sems = [pltpu.SemaphoreType.DMA((n_harm,)) for _ in range(12)]
    lensed = pl.pallas_call(
        functools.partial(sky_step, n_harm, n_remap, per_dev),
        grid=(groups,),
        in_specs=[
            pl.BlockSpec((per_group, 1, rows, depth), lambda g: (0, g, 0, 0)),
            pl.BlockSpec((per_group, 1, cycles, depth), lambda g: (0, g, 0, 0)),
        ]
        + [whole] * 7,
        out_specs=whole,
        out_shape=jax.ShapeDtypeStruct((sims, quarter), jnp.bfloat16),
        scratch_shapes=[
            pltpu.VMEM((rows * cycles, LANES), jnp.float32),
            pltpu.VMEM((rows * cycles, LANES), jnp.float32),
            pltpu.VMEM((n_remap * n_harm * piece, LANES), jnp.float32),
            pltpu.VMEM((n_harm, 4, tiles, LANES), jnp.int32),
            pltpu.VMEM((2, cycles * LANES, 2 * LANES), jnp.bfloat16),
            pltpu.VMEM((tiles + 16, cycles * LANES), jnp.float32),
            pltpu.VMEM((per_dev, 2, cycles, tiles, LANES), jnp.float32),
            pltpu.VMEM((cycles, per_dev * tiles, LANES), jnp.float32),
            pltpu.VMEM((n_harm, per_dev * tiles, LANES), jnp.float32),
        ]
        + sems,
        compiler_params=pltpu.CompilerParams(
            collective_id=0, has_side_effects=True, vmem_limit_bytes=56 * 2**20
        ),
    )(
        alm.reshape(per_group, groups, rows, depth),
        legendre.reshape(per_group, groups, cycles, depth),
        *(array.reshape(tiles, LANES) for array in (src_cycle, src_phi, off_cycle, off_phi)),
        jnp.asarray(first_table.astype(np.float32)),
        jnp.asarray(twist),
        jnp.asarray(second_table.astype(np.float32)),
    )
    return lensed.reshape(sims, 1, quarter)


def fits(mesh, alm, legendre, src_cycle):
    n_harm, n_remap = mesh.shape["harm"], mesh.shape["remap"]
    cycles = legendre.shape[1]
    sims = alm.shape[1] // 2
    phi_count = src_cycle.shape[1]
    return (
        cycles == n_harm == 8
        and sims % n_harm == 0
        and alm.shape[0] == LANES * n_harm * n_remap
        and phi_count == LANES * 64
        and (phi_count // n_remap) % (16 * LANES) == 0
        and (n_harm * n_remap) % 8 == 0
        and n_remap == 4
    )


def solution(mesh):
    def run(*arrays):
        chosen = body if fits(mesh, arrays[0], arrays[1], arrays[2]) else general_body
        return sharded(mesh, chosen)(*arrays)

    return run


def sharded(mesh, chosen):
    return jax.shard_map(
        chosen,
        mesh=mesh,
        in_specs=(
            P(("harm", "remap"), None, None),
            P(("harm", "remap"), None, None),
            P("harm", "remap"),
            P("harm", "remap"),
            P("harm", "remap"),
            P("harm", "remap"),
        ),
        out_specs=P(None, "harm", "remap"),
        check_vma=False,
    )
```
